128 devices in a mesh: dp: 16 (over z_hi, x, core), fsdp: 8 (over y, z_lo).
Axes of the slice: x: 4, y: 4, z: 4 (z_hi: 2, z_lo: 2; z = z_hi * 2 + z_lo), core: 2. Of those that a mesh axis runs over, the one named last changes fastest.
Arguments:
- layer_input: bfloat16 [65536, 8192], P(('dp', 'fsdp')), may hold values from -400 to 400
- rotated_grad: bfloat16 [65536, 512], P(('dp', 'fsdp')), may hold values from -24 to 24
- norm_gain: bfloat16 [8192], replicated, may hold values from 0.099609375 to 1.8984375
- key_weight: bfloat16 [8192, 512], P('fsdp'), may hold values from -3 to 3
- block_length: int32 [8, 16, 16], P('fsdp'), may hold values from 1 to 64, as said below
- block_owner: int32 [8, 16, 16], P('fsdp'), may hold values from 0 to 15, as said below
- block_source_offset: int32 [8, 16, 16], P('fsdp'), may hold values from 0 to 511, as said below
- block_pack_offset: int32 [8, 16, 16], P('fsdp'), may hold values from 0 to 511, as said below
- block_position: int32 [8, 16, 16], P('fsdp'), may hold values from 0 to 8128
Outputs:
- input_grad: bfloat16 [65536, 8192], P(('dp', 'fsdp'))
- weight_grad: float32 [8192, 512], P(('dp', 'fsdp'))
The draws below stay inside these ranges and needn't reach their ends.
Inputs may be any that keep to these rules, and one draw needn't show every extreme that they name: `block_length`: in each column every loader shard holds 16 blocks that tile its 512 rows, one block for each pack owner; every owner receives one block from each loader shard of its column, and these tile its 512 rows. Every loader shard has one block of exactly 64 rows, and every owner receives one such block. `block_owner`: for each loader shard, the owners of its blocks are all different. `block_source_offset`: running sums of the lengths of a loader shard's blocks, in block order. `block_pack_offset`: blocks arriving at one owner do not intersect.
All inputs are finite; a program needn't handle non-finite values.
Results may differ from the reference program's by a relative error of at most 0.014.
Values may be sent and summed in bfloat16 or wider, within the bound.
No kernel may reach another device: no remote copies, remote signals or barrier semaphores. Data moves between devices by JAX's collectives and lax.ppermute only.
A program may use at most 128 MiB of HBM per device.

```python
import math
import jax
import jax.numpy as jnp
from jax import lax

D = 8192
HEAD = 128
CONTEXT = 8192
KV_HEADS = 4
TOK_DEV = 512
KV = 512
CAP = 64
LOADERS = 16
COLUMNS = 8
TOKENS = 65536


def block_tables(key):
    loaders = LOADERS
    capacity = CAP
    rest = TOK_DEV - capacity
    step_size = rest // (loaders - 1)
    extra = rest % (loaders - 1)

    def permute_one(small_key):
        return jax.random.permutation(small_key, loaders)

    def one_column(column_key):
        keys = jax.random.split(column_key, 6)
        index = jnp.arange(loaders - 1, dtype=jnp.int32)
        spread = jax.random.randint(keys[0], (loaders // 2,), 0, step_size)
        paired = spread[index // 2]
        sign_pair = jnp.where(index % 2 == 0, 1, -1).astype(jnp.int32)
        lonely = ((index == loaders - 2) & ((loaders - 1) % 2 == 1)).astype(jnp.int32)
        others = step_size + (index < extra).astype(jnp.int32) + sign_pair * paired * (1 - lonely)
        base = jnp.concatenate([jnp.full((1,), capacity, jnp.int32), others.astype(jnp.int32)])
        base = jax.random.permutation(keys[1], base)
        sigma = jax.random.permutation(keys[2], loaders)
        tau = jax.random.permutation(keys[3], loaders)
        order = jax.vmap(permute_one)(jax.random.split(keys[4], loaders))
        owner = sigma[(tau[:, None] + order) % loaders]
        length = base[order]
        source_offset = jnp.cumsum(length, axis=1) - length
        shard_ids = jnp.arange(loaders, dtype=jnp.int32)
        to_owner = (owner[:, :, None] == shard_ids[None, None, :]).astype(jnp.int32)
        matrix = jnp.sum(length[:, :, None] * to_owner, axis=1)
        rank = jax.vmap(permute_one)(jax.random.split(keys[5], loaders))
        rank_sd = rank.T
        earlier = (rank_sd[:, None, :] < rank_sd[None, :, :]).astype(jnp.int32)
        pack_start = jnp.sum(matrix[:, None, :] * earlier, axis=0)
        pack_offset = jnp.sum(pack_start[:, None, :] * to_owner, axis=2)
        return (length.astype(jnp.int32), owner.astype(jnp.int32), source_offset.astype(jnp.int32), pack_offset.astype(jnp.int32))
    return jax.vmap(one_column)(jax.random.split(key, COLUMNS))


def shared_direction(key):
    direction = jax.random.truncated_normal(jax.random.fold_in(key, 11), -2.8, 2.8, (D,), jnp.float32)
    column = jax.random.randint(jax.random.fold_in(key, 13), (), 0, KV)
    return (direction, column)


def draw_block_length(key, part):
    return block_tables(key)[0]


def draw_block_owner(key, part):
    return block_tables(key)[1]


def draw_block_source_offset(key, part):
    return block_tables(key)[2]


def draw_block_pack_offset(key, part):
    return block_tables(key)[3]


def draw_block_position(key, part):
    key = jax.random.fold_in(key, 7)
    first_key, second_key = jax.random.split(key)
    shape = (COLUMNS, LOADERS, LOADERS)
    values = jax.random.randint(first_key, shape, 0, CONTEXT - CAP + 1)
    spot = jax.random.randint(second_key, (), 0, COLUMNS * LOADERS * LOADERS)
    flat = jnp.arange(COLUMNS * LOADERS * LOADERS, dtype=jnp.int32).reshape(shape)
    return jnp.where(flat == spot, CONTEXT - CAP, values).astype(jnp.int32)


def draw_key_weight(key, part):
    direction, column = shared_direction(key)
    key = jax.random.fold_in(key, 5)
    entries = jax.random.truncated_normal(key, -6.0, 6.0, (D, KV), jnp.float32) / math.sqrt(KV)
    column_ids = jnp.arange(KV, dtype=jnp.int32)[None, :]
    values = jnp.where(column_ids == column, direction[:, None], entries)
    return values.astype(jnp.bfloat16)


def draw_layer_input(key, part):
    direction, column = shared_direction(key)
    key = jax.random.fold_in(key, 3)
    keys = jax.random.split(key, 5)
    col_scale = jnp.exp(jax.random.uniform(keys[2], (1, D), jnp.float32, 0.0, math.log(10.0)))
    row_sign = (2 * jax.random.randint(keys[4], (TOKENS, 1), 0, 2) - 1).astype(jnp.float32)
    aligned = row_sign * direction[None, :]
    row_scale = jnp.exp(jax.random.uniform(keys[1], (TOKENS, 1), jnp.float32, 0.0, math.log(10.0)))
    noise = jax.random.truncated_normal(keys[0], -2.8, 2.8, (TOKENS, D), jnp.float32)
    values = (noise + aligned) * 0.7071 * row_scale * col_scale
    return values.astype(jnp.bfloat16)


def shard_levels(own_key, dims, shards, least, top_value):
    loudness, own = 1.0, jax.random.fold_in(own_key, 6)
    for dim, blocks in shards:
        steps = jnp.exp(jax.random.uniform(jax.random.fold_in(own, dim), (blocks,), jnp.float32, least / len(shards), top_value / len(shards)))
        loudness = loudness * jnp.repeat(steps, dims[dim] // blocks).reshape([-1 if axis == dim else 1 for axis in range(len(dims))])
    return loudness


def scatter_about(own_key, extent, width, bound, cuts=(), kind=jnp.bfloat16):
    drawn = jax.random.normal(own_key, extent, jnp.float32) * width
    if len(cuts) > 0:
        drawn = shard_levels(own_key, extent, cuts, -0.22, 0.18) * drawn
    return jnp.clip(drawn, min=-bound, max=bound).astype(kind)


def setup_inputs(seed: int = 0) -> dict:
    key_of = jax.random.split(jax.random.key(seed), 10)
    return {
        "layer_input": draw_layer_input(jax.random.fold_in(key_of[9], 71), 0),
        "rotated_grad": scatter_about(key_of[1], (TOKENS, KV), 4.0, 24.0, ((0, 128),)),
        "norm_gain": jnp.clip(1.0 + 0.18 * jax.random.normal(key_of[2], (D,), jnp.float32), 0.099609375, 1.8984375).astype(jnp.bfloat16),
        "key_weight": draw_key_weight(jax.random.fold_in(key_of[9], 71), 0),
        "block_length": draw_block_length(jax.random.fold_in(key_of[9], 71), 0),
        "block_owner": draw_block_owner(jax.random.fold_in(key_of[9], 71), 0),
        "block_source_offset": draw_block_source_offset(jax.random.fold_in(key_of[9], 71), 0),
        "block_pack_offset": draw_block_pack_offset(jax.random.fold_in(key_of[9], 71), 0),
        "block_position": draw_block_position(jax.random.fold_in(key_of[9], 71), 0),
    }


rope_base = 500000.0
norm_eps = 1e-05

def pack_tables(block_length, block_owner, block_source_offset, block_pack_offset, block_position):
    shard_ids = jnp.arange(LOADERS, dtype=jnp.int32)
    chosen = (block_owner[:, None, :, :] == shard_ids[None, :, None, None]).astype(jnp.int32)
    start = lax.optimization_barrier(jnp.sum(chosen * block_pack_offset[:, None], axis=3))
    length = lax.optimization_barrier(jnp.sum(chosen * block_length[:, None], axis=3))
    source_start = lax.optimization_barrier(jnp.sum(chosen * block_source_offset[:, None], axis=3))
    first_pos = lax.optimization_barrier(jnp.sum(chosen * block_position[:, None], axis=3))
    row_ids = jnp.arange(TOK_DEV, dtype=jnp.int32)
    lower = row_ids[None, None, :, None] >= start[:, :, None, :]
    upper = row_ids[None, None, :, None] < (start + length)[:, :, None, :]
    inside = (lower & upper).astype(jnp.int32)
    source = lax.optimization_barrier(jnp.sum(inside * shard_ids[None, None, None, :], axis=3))
    first = lax.optimization_barrier(jnp.sum(inside * start[:, :, None, :], axis=3))
    base_row = lax.optimization_barrier(jnp.sum(inside * source_start[:, :, None, :], axis=3))
    base_pos = lax.optimization_barrier(jnp.sum(inside * first_pos[:, :, None, :], axis=3))
    offset = row_ids[None, None, :] - first
    column_ids = jnp.arange(COLUMNS, dtype=jnp.int32)[:, None, None]
    loader_row = (source * COLUMNS + column_ids) * TOK_DEV + base_row + offset
    position = base_pos + offset
    loader_row = jnp.transpose(loader_row, (1, 0, 2)).reshape(LOADERS * COLUMNS, TOK_DEV)
    position = jnp.transpose(position, (1, 0, 2)).reshape(LOADERS * COLUMNS, TOK_DEV)
    return (loader_row.astype(jnp.int32), position.astype(jnp.int32))

def rope_back(rotated, position):
    half_head = HEAD // 2
    exponent = jnp.arange(half_head, dtype=jnp.float32) * (2.0 / HEAD)
    inverse = jnp.power(jnp.float32(rope_base), -exponent)
    angle = position.astype(jnp.float32)[:, None] * inverse[None, :]
    cosine = jnp.cos(angle)[:, None, :]
    sine = jnp.sin(angle)[:, None, :]
    grads = rotated.astype(jnp.float32).reshape(-1, KV_HEADS, HEAD)
    first_half = grads[..., :half_head]
    second_half = grads[..., half_head:]
    joined = jnp.concatenate([first_half * cosine + second_half * sine, second_half * cosine - first_half * sine], axis=-1)
    return joined.reshape(-1, KV_HEADS * HEAD).astype(jnp.bfloat16)

def recompute_norm(packed, gain):
    values = packed.astype(jnp.float32)
    inv_rms = lax.rsqrt(lax.optimization_barrier(jnp.mean(values * values, axis=-1, keepdims=True)) + norm_eps)
    normed = (values * inv_rms * gain.astype(jnp.float32)[None, :]).astype(jnp.bfloat16)
    return (values, inv_rms, normed)

def input_gradient(values, inv_rms, gain, delta):
    scaled = delta * gain.astype(jnp.float32)[None, :]
    inner = lax.optimization_barrier(jnp.mean(scaled * values, axis=-1, keepdims=True))
    return (inv_rms * (scaled - values * inv_rms * inv_rms * inner)).astype(jnp.bfloat16)

def reference(layer_input, rotated_grad, norm_gain, key_weight, block_length, block_owner, block_source_offset, block_pack_offset, block_position):
    loader_rows, positions = pack_tables(block_length, block_owner, block_source_offset, block_pack_offset, block_position)
    scale = 1.0 / math.sqrt(TOKENS)

    def per_device(total, inputs):
        loader_row, position, rotated = inputs
        packed = jnp.take(layer_input, loader_row, axis=0)
        values, inv_rms, normed = recompute_norm(packed, norm_gain)
        key_grad = rope_back(rotated, position)
        delta = jnp.dot(key_grad, key_weight.T, preferred_element_type=jnp.float32)
        grad_rows = input_gradient(values, inv_rms, norm_gain, delta)
        term = jnp.dot(normed.T, key_grad, preferred_element_type=jnp.float32) * scale
        rounded = lax.optimization_barrier(term.astype(jnp.bfloat16)).astype(jnp.float32)
        return (total + rounded, grad_rows)
    stacked = rotated_grad.reshape(LOADERS * COLUMNS, TOK_DEV, KV)
    total, grad_rows = lax.scan(per_device, jnp.zeros((D, KV), jnp.float32), (loader_rows, positions, stacked))
    return (grad_rows.reshape(TOKENS, D), total)
```

```python
import math

import jax
import jax.numpy as jnp
from jax import lax
from jax.sharding import PartitionSpec as P

HEAD = 128
KV_HEADS = 4
AXES = ("dp", "fsdp")

rope_base = 500000.0
norm_eps = 1e-05


def place(zh, x, c, y, zl):
    return ((((zh % 2) * 4 + x % 4) * 2 + c % 2) * 4 + y % 4) * 2 + zl % 2


def perm(step):
    pairs = []
    for zh in range(2):
        for x in range(4):
            for c in range(2):
                for y in range(4):
                    for zl in range(2):
                        pairs.append((place(zh, x, c, y, zl), place(*step(zh, x, c, y, zl))))
    return pairs


def along_core(v):
    return lax.ppermute(v, AXES, perm(lambda zh, x, c, y, zl: (zh, x, c + 1, y, zl)))


def along_x(v, n):
    return lax.ppermute(v, AXES, perm(lambda zh, x, c, y, zl: (zh, x + n, c, y, zl)))


def along_y(v, n):
    return lax.ppermute(v, AXES, perm(lambda zh, x, c, y, zl: (zh, x, c, y + n, zl)))


def along_z(v, n):
    def step(zh, x, c, y, zl):
        z = (zh * 2 + zl + n) % 4
        return (z // 2, x, c, y, z % 2)

    return lax.ppermute(v, AXES, perm(step))


def swap_zlo(v):
    return lax.ppermute(v, AXES, perm(lambda zh, x, c, y, zl: (zh, x, c, y, zl + 1)))


def pick(v, i, axis=0):
    return lax.dynamic_index_in_dim(v, i, axis, keepdims=False)


def rope_back(rotated, position):
    half_head = HEAD // 2
    exponent = jnp.arange(half_head, dtype=jnp.float32) * (2.0 / HEAD)
    inverse = jnp.power(jnp.float32(rope_base), -exponent)
    angle = position.astype(jnp.float32)[:, None] * inverse[None, :]
    cosine = jnp.cos(angle)
    sine = jnp.sin(angle)
    cos_full = jnp.concatenate([cosine, cosine] * KV_HEADS, axis=1)
    sin_full = jnp.concatenate([sine, -sine] * KV_HEADS, axis=1)
    grads = rotated.astype(jnp.float32)
    halves = [grads[:, i * half_head : (i + 1) * half_head] for i in range(2 * KV_HEADS)]
    swapped = jnp.concatenate([halves[i ^ 1] for i in range(2 * KV_HEADS)], axis=1)
    return (grads * cos_full + swapped * sin_full).astype(jnp.bfloat16)


def body(
    layer_input,
    rotated_grad,
    norm_gain,
    key_weight,
    block_length,
    block_owner,
    block_source_offset,
    block_pack_offset,
    block_position,
):
    tok_rows, width = layer_input.shape
    kv = rotated_grad.shape[1]
    loaders = lax.axis_size("dp")
    columns = lax.axis_size("fsdp")
    dp = lax.axis_index("dp")
    fs = lax.axis_index("fsdp")
    zh, xx, core = dp // 8, (dp // 2) % 4, dp % 2
    yy, zl = fs // 2, fs % 2
    zz = zh * 2 + zl
    capacity = 2 * tok_rows // loaders
    lengths = block_length[0]
    owners = block_owner[0]
    source_offsets = block_source_offset[0]
    pack_offsets = block_pack_offset[0]
    positions = block_position[0]
    shard_ids = jnp.arange(loaders, dtype=jnp.int32)
    slot_ids = jnp.arange(capacity, dtype=jnp.int32)
    row_ids = jnp.arange(tok_rows, dtype=jnp.int32)

    mine = (owners == dp).astype(jnp.int32)
    arrive_start = jnp.sum(mine * pack_offsets, axis=1)
    arrive_length = jnp.sum(mine * lengths, axis=1)
    arrive_position = jnp.sum(mine * positions, axis=1)
    inside = (
        (row_ids[:, None] >= arrive_start[None, :])
        & (row_ids[:, None] < (arrive_start + arrive_length)[None, :])
    ).astype(jnp.int32)
    position = row_ids + jnp.sum(inside * (arrive_position - arrive_start)[None, :], axis=1)

    chosen = (pick(owners, dp)[None, :] == shard_ids[:, None]).astype(jnp.int32)
    send_start = jnp.sum(chosen * pick(source_offsets, dp)[None, :], axis=1)
    send_length = jnp.sum(chosen * pick(lengths, dp)[None, :], axis=1)

    def spread(start, length):
        row = jnp.where(slot_ids[None, :] < length[:, None], start[:, None] + slot_ids[None, :], -1)
        return (row.reshape(-1)[:, None] == row_ids[None, :]).astype(jnp.bfloat16)

    to_owner = spread(send_start, send_length)
    to_loader = spread(arrive_start, arrive_length)

    def move(matrix, rows):
        return jnp.dot(matrix, rows, preferred_element_type=jnp.float32).astype(jnp.bfloat16)

    def place_rows(matrix, rows):
        return lax.dot_general(
            matrix, rows, (((0,), (0,)), ((), ())), preferred_element_type=jnp.float32
        ).astype(jnp.bfloat16)

    def exchange(rows):
        blocks = rows.reshape(loaders, capacity, rows.shape[1])
        return lax.all_to_all(blocks, "dp", split_axis=0, concat_axis=0, tiled=True).reshape(rows.shape)

    key_grad = rope_back(rotated_grad, position)
    key_back = exchange(move(to_loader, key_grad))
    arrived = exchange(move(to_owner, layer_input))
    key_loader = place_rows(to_owner, key_back)

    depth = key_weight.shape[0] // 2
    half = pick(key_weight.reshape(2, depth, kv), core)
    other = swap_zlo(half)
    pair = jnp.where(zl == 0, jnp.stack([half, other]), jnp.stack([other, half]))
    whole = jnp.zeros((4, 2, depth, kv), jnp.bfloat16)
    whole = lax.dynamic_update_index_in_dim(whole, pair, yy, 0)
    for n in (1, 3, 2):
        whole = lax.dynamic_update_index_in_dim(whole, along_y(pair, n), (yy - n) % 4, 0)
    swapped = along_core(whole)
    weight = jnp.where(core == 0, jnp.stack([whole, swapped], 2), jnp.stack([swapped, whole], 2))
    weight = weight.reshape(width, kv)

    gain = norm_gain.astype(jnp.float32)[None, :]
    own = layer_input.astype(jnp.float32)
    own_rms = lax.rsqrt(jnp.mean(own * own, axis=-1, keepdims=True) + norm_eps)
    normed = (own * own_rms * gain).astype(jnp.bfloat16)
    scale = 1.0 / math.sqrt(tok_rows * loaders * columns)
    term = (
        lax.dot_general(normed, key_loader, (((0,), (0,)), ((), ())), preferred_element_type=jnp.float32)
        * scale
    ).astype(jnp.bfloat16)
    rows = width // (loaders * columns)
    term = term.reshape(8, 2, 8 * rows, kv)
    got = along_core(pick(term, 1 - core, 1))
    part = (pick(term, core, 1).astype(jnp.float32) + got.astype(jnp.float32)).astype(jnp.bfloat16)

    def reduce(part, axis, me, send):
        total = pick(part, me, axis).astype(jnp.float32)
        for n in (1, 3, 2):
            total = total + send(pick(part, (me + n) % 4, axis), n).astype(jnp.float32)
        return total

    part = reduce(part.reshape(8, 4, 2 * rows, kv), 1, yy, along_y).astype(jnp.bfloat16)
    part = part.reshape(2, 4, 2, rows, kv).transpose(0, 2, 1, 3, 4).reshape(4, 4, rows, kv)
    part = reduce(part, 0, zz, along_z).astype(jnp.bfloat16)
    weight_grad = reduce(part, 0, xx, along_x)

    packed = place_rows(to_loader, arrived)
    values = packed.astype(jnp.float32)
    inv_rms = lax.rsqrt(jnp.mean(values * values, axis=-1, keepdims=True) + norm_eps)
    input_delta = lax.dot_general(
        key_grad, weight, (((1,), (1,)), ((), ())), preferred_element_type=jnp.float32
    )
    scaled = input_delta * gain
    inner = jnp.mean(scaled * values, axis=-1, keepdims=True)
    input_grad = (inv_rms * (scaled - values * inv_rms * inv_rms * inner)).astype(jnp.bfloat16)
    return (input_grad, weight_grad)


def solution(mesh):
    return jax.shard_map(
        body,
        mesh=mesh,
        in_specs=(
            P(("dp", "fsdp"), None),
            P(("dp", "fsdp"), None),
            P(),
            P("fsdp", None),
            P("fsdp", None, None),
            P("fsdp", None, None),
            P("fsdp", None, None),
            P("fsdp", None, None),
            P("fsdp", None, None),
        ),
        out_specs=(P(("dp", "fsdp"), None), P(("dp", "fsdp"), None)),
        check_vma=False,
    )
```

```python
import functools
import math

import jax
import jax.numpy as jnp
from jax import lax
from jax.experimental import pallas as pl
from jax.experimental.pallas import tpu as pltpu
from jax.sharding import PartitionSpec as P

HEAD = 128
KV_HEADS = 4
AXES = ("dp", "fsdp")

rope_base = 500000.0
norm_eps = 1e-05


def place(zh, x, c, y, zl):
    return ((((zh % 2) * 4 + x % 4) * 2 + c % 2) * 4 + y % 4) * 2 + zl % 2


def perm(step):
    pairs = []
    for zh in range(2):
        for x in range(4):
            for c in range(2):
                for y in range(4):
                    for zl in range(2):
                        pairs.append((place(zh, x, c, y, zl), place(*step(zh, x, c, y, zl))))
    return pairs


def along_core(v):
    return lax.ppermute(v, AXES, perm(lambda zh, x, c, y, zl: (zh, x, c + 1, y, zl)))


def along_x(v, n):
    return lax.ppermute(v, AXES, perm(lambda zh, x, c, y, zl: (zh, x + n, c, y, zl)))


def along_y(v, n):
    return lax.ppermute(v, AXES, perm(lambda zh, x, c, y, zl: (zh, x, c, y + n, zl)))


def along_z(v, n):
    def step(zh, x, c, y, zl):
        z = (zh * 2 + zl + n) % 4
        return (z // 2, x, c, y, z % 2)

    return lax.ppermute(v, AXES, perm(step))


def swap_zlo(v):
    return lax.ppermute(v, AXES, perm(lambda zh, x, c, y, zl: (zh, x, c, y, zl + 1)))


def pick(v, i, axis=0):
    return lax.dynamic_index_in_dim(v, i, axis, keepdims=False)


def rope_tables(position):
    half_head = HEAD // 2
    exponent = jnp.arange(half_head, dtype=jnp.float32) * (2.0 / HEAD)
    inverse = jnp.power(jnp.float32(rope_base), -exponent)
    angle = position.astype(jnp.float32)[:, None] * jnp.concatenate([inverse, inverse])[None, :]
    sign = jnp.where(jnp.arange(HEAD) < half_head, 1.0, -1.0).astype(jnp.float32)
    return jnp.cos(angle), jnp.sin(angle) * sign[None, :]


def one_hot(select, count):
    lanes = lax.broadcasted_iota(jnp.int32, (select.shape[0], count), 1)
    return (select == lanes).astype(jnp.float32).astype(jnp.bfloat16)


def rope_kernel(select_ref, cos_ref, sin_ref, rotated_ref, key_ref, out_ref):
    cosine, sine = cos_ref[...], sin_ref[...]
    for head in range(KV_HEADS):
        cols = slice(head * HEAD, (head + 1) * HEAD)
        grads = rotated_ref[:, cols].astype(jnp.float32)
        turned = pltpu.roll(grads, HEAD // 2, 1)
        key_ref[:, cols] = (grads * cosine + turned * sine).astype(jnp.bfloat16)
    spread = one_hot(select_ref[...], key_ref.shape[0])
    out_ref[...] = jnp.dot(spread, key_ref[...], preferred_element_type=jnp.float32).astype(jnp.bfloat16)


def rope_and_spread(select, cosine, sine, rotated, beside):
    rows, kv = rotated.shape
    slots = select.shape[0]
    whole = lambda j: (0, 0)
    return pl.pallas_call(
        rope_kernel,
        grid=(1,),
        in_specs=[pl.BlockSpec(v.shape, whole) for v in (select, cosine, sine, rotated)],
        out_specs=[pl.BlockSpec((rows, kv), whole), pl.BlockSpec((slots, kv), lambda j: (0, beside // kv))],
        out_shape=(
            jax.ShapeDtypeStruct((rows, kv), jnp.bfloat16),
            jax.ShapeDtypeStruct((slots, beside + kv), jnp.bfloat16),
        ),
        cost_estimate=pl.CostEstimate(flops=2 * slots * rows * kv, bytes_accessed=4 << 20, transcendentals=0),
        compiler_params=pltpu.CompilerParams(vmem_limit_bytes=58 << 20),
        name="rope_and_spread",
    )(select, cosine, sine, rotated)


BLOCK = 1024


def spread_kernel(select_ref, rows_ref, *rest):
    out_ref, spread = rest[-2:]

    @pl.when(pl.program_id(0) == 0)
    def _():
        spread[...] = one_hot(select_ref[...], spread.shape[1])

    out_ref[...] = jnp.dot(spread[...], rows_ref[...], preferred_element_type=jnp.float32).astype(jnp.bfloat16)


def spread_rows(select, rows, first, width, beside=None):
    slots, count = select.shape[0], rows.shape[0]
    given = [] if beside is None else [beside]
    total = width if beside is None else beside.shape[1]
    return pl.pallas_call(
        spread_kernel,
        grid=(width // BLOCK,),
        in_specs=[
            pl.BlockSpec((slots, 1), lambda j: (0, 0)),
            pl.BlockSpec((count, BLOCK), lambda j: (0, first // BLOCK + j)),
        ]
        + [pl.BlockSpec(memory_space=pl.ANY)] * len(given),
        out_specs=pl.BlockSpec((slots, BLOCK), lambda j: (0, j)),
        out_shape=jax.ShapeDtypeStruct((slots, total), jnp.bfloat16),
        input_output_aliases={2: 0} if given else {},
        scratch_shapes=[pltpu.VMEM((slots, count), jnp.bfloat16)],
        cost_estimate=pl.CostEstimate(
            flops=2 * slots * count * width, bytes_accessed=2 * (slots + count) * width, transcendentals=0
        ),
        compiler_params=pltpu.CompilerParams(vmem_limit_bytes=58 << 20),
        name="spread_rows",
    )(select, rows, *given)


def lane_sums(values):
    total = values[:, :128]
    for k in range(1, values.shape[1] // 128):
        total = total + values[:, k * 128 : (k + 1) * 128]
    return total


def delta_times_gain(key, weight, gain):
    return lax.dot_general(key, weight, (((1,), (1,)), ((), ())), preferred_element_type=jnp.float32) * gain


def first_pass_kernel(
    core_ref, select_ref, arrived_ref, key_ref, mine_ref, other_ref, gain_ref, square_in, inner_in, *rest
):
    packed_ref, square_ref, inner_ref, gather = rest[-4:]

    @pl.when(pl.program_id(0) == 0)
    def _():
        gather[...] = one_hot(select_ref[...], gather.shape[1])
        square_ref[...] = square_in[...]
        inner_ref[...] = inner_in[...]

    values = jnp.dot(gather[...], arrived_ref[...], preferred_element_type=jnp.float32)
    packed_ref[...] = values.astype(jnp.bfloat16)
    square_ref[...] += lane_sums(values * values)
    depth = mine_ref.shape[1]
    core = core_ref[0]
    for half, weight_ref in ((core, mine_ref), (1 - core, other_ref)):
        cols = pl.ds(pl.multiple_of(half * depth, depth), depth)
        scaled = delta_times_gain(key_ref[...], weight_ref[0], gain_ref[:, cols])
        inner_ref[...] += lane_sums(scaled * packed_ref[:, cols].astype(jnp.float32))


def first_pass(core, select, arrived, key_grad, mine, other, gain, square, inner, packed, first, part, width):
    rows, kv = key_grad.shape
    slots = arrived.shape[0]
    depth = mine.shape[1]
    base = first // BLOCK
    whole = lambda j, core: (0, 0)
    column = lambda j, core: (0, base + j)
    deep = lambda j, core: (base + j, 0, 0)
    sums = jax.ShapeDtypeStruct((rows, 128), jnp.float32)
    operands = [core, select, arrived, key_grad, mine, other, gain, square, inner]
    in_specs = [
        pl.BlockSpec((rows, 1), whole),
        pl.BlockSpec((slots, BLOCK), lambda j, core: (0, j)),
        pl.BlockSpec((rows, kv), whole),
        pl.BlockSpec((1, depth, kv), deep),
        pl.BlockSpec((1, depth, kv), deep),
        pl.BlockSpec((1, BLOCK), column),
        pl.BlockSpec((rows, 128), whole),
        pl.BlockSpec((rows, 128), whole),
    ]
    aliases = {}
    if packed is not None:
        operands.append(packed)
        in_specs.append(pl.BlockSpec(memory_space=pl.ANY))
        aliases = {9: 0}
    return pl.pallas_call(
        first_pass_kernel,
        grid_spec=pltpu.PrefetchScalarGridSpec(
            num_scalar_prefetch=1,
            grid=(part // BLOCK,),
            in_specs=in_specs,
            out_specs=[
                pl.BlockSpec((rows, BLOCK), column),
                pl.BlockSpec((rows, 128), whole),
                pl.BlockSpec((rows, 128), whole),
            ],
            scratch_shapes=[pltpu.VMEM((rows, slots), jnp.bfloat16)],
        ),
        out_shape=(jax.ShapeDtypeStruct((rows, width), jnp.bfloat16), sums, sums),
        input_output_aliases=aliases,
        cost_estimate=pl.CostEstimate(
            flops=2 * rows * (slots + kv) * part,
            bytes_accessed=2 * (slots + rows + kv) * part,
            transcendentals=0,
        ),
        compiler_params=pltpu.CompilerParams(vmem_limit_bytes=58 << 20),
        name="first_pass",
    )(*operands)


def second_pass_kernel(
    core_ref, packed_ref, key_ref, mine_ref, other_ref, gain_ref, square_ref, inner_ref, out_ref, inv, coef, *, width
):
    @pl.when(pl.program_id(0) == 0)
    def _():
        square = jnp.sum(square_ref[...], axis=1, keepdims=True) * (1.0 / width)
        inner = jnp.sum(inner_ref[...], axis=1, keepdims=True) * (1.0 / width)
        inverse = lax.rsqrt(square + norm_eps)
        inv[...] = inverse
        coef[...] = inverse * inverse * inner

    depth = mine_ref.shape[1]
    core = core_ref[0]
    for half, weight_ref in ((core, mine_ref), (1 - core, other_ref)):
        cols = pl.ds(pl.multiple_of(half * depth, depth), depth)
        scaled = delta_times_gain(key_ref[...], weight_ref[0], gain_ref[:, cols])
        values = packed_ref[:, cols].astype(jnp.float32)
        out_ref[:, cols] = (inv[...] * (scaled - values * coef[...])).astype(jnp.bfloat16)


def second_pass(core, packed, key_grad, mine, other, gain, square, inner):
    rows, kv = key_grad.shape
    width = packed.shape[1]
    depth = mine.shape[1]
    whole = lambda j, core: (0, 0)
    column = lambda j, core: (0, j)
    deep = lambda j, core: (j, 0, 0)
    return pl.pallas_call(
        functools.partial(second_pass_kernel, width=width),
        grid_spec=pltpu.PrefetchScalarGridSpec(
            num_scalar_prefetch=1,
            grid=(width // BLOCK,),
            in_specs=[
                pl.BlockSpec((rows, BLOCK), column),
                pl.BlockSpec((rows, kv), whole),
                pl.BlockSpec((1, depth, kv), deep),
                pl.BlockSpec((1, depth, kv), deep),
                pl.BlockSpec((1, BLOCK), column),
                pl.BlockSpec((rows, 128), whole),
                pl.BlockSpec((rows, 128), whole),
            ],
            out_specs=pl.BlockSpec((rows, BLOCK), column),
            scratch_shapes=[pltpu.VMEM((rows, 1), jnp.float32), pltpu.VMEM((rows, 1), jnp.float32)],
        ),
        out_shape=jax.ShapeDtypeStruct((rows, width), jnp.bfloat16),
        cost_estimate=pl.CostEstimate(
            flops=2 * rows * kv * width, bytes_accessed=2 * (2 * rows + kv) * width, transcendentals=0
        ),
        compiler_params=pltpu.CompilerParams(vmem_limit_bytes=58 << 20),
        name="second_pass",
    )(core, packed, key_grad, mine, other, gain, square, inner)


CHUNKS = (3072, 5120)


def body(
    layer_input,
    rotated_grad,
    norm_gain,
    key_weight,
    block_length,
    block_owner,
    block_source_offset,
    block_pack_offset,
    block_position,
):
    tok_rows, width = layer_input.shape
    kv = rotated_grad.shape[1]
    loaders = lax.axis_size("dp")
    columns = lax.axis_size("fsdp")
    dp = lax.axis_index("dp")
    fs = lax.axis_index("fsdp")
    zh, xx, core = dp // 8, (dp // 2) % 4, dp % 2
    yy, zl = fs // 2, fs % 2
    zz = zh * 2 + zl
    capacity = 2 * tok_rows // loaders
    lengths = block_length[0]
    owners = block_owner[0]
    source_offsets = block_source_offset[0]
    pack_offsets = block_pack_offset[0]
    positions = block_position[0]
    shard_ids = jnp.arange(loaders, dtype=jnp.int32)
    slot_ids = jnp.arange(capacity, dtype=jnp.int32)
    row_ids = jnp.arange(tok_rows, dtype=jnp.int32)

    mine = (owners == dp).astype(jnp.int32)
    arrive_start = jnp.sum(mine * pack_offsets, axis=1)
    arrive_length = jnp.sum(mine * lengths, axis=1)
    arrive_position = jnp.sum(mine * positions, axis=1)
    inside = (
        (row_ids[:, None] >= arrive_start[None, :])
        & (row_ids[:, None] < (arrive_start + arrive_length)[None, :])
    ).astype(jnp.int32)
    position = row_ids + jnp.sum(inside * (arrive_position - arrive_start)[None, :], axis=1)
    slot = row_ids + jnp.sum(inside * (shard_ids * capacity - arrive_start)[None, :], axis=1)

    chosen = (pick(owners, dp)[None, :] == shard_ids[:, None]).astype(jnp.int32)
    send_start = jnp.sum(chosen * pick(source_offsets, dp)[None, :], axis=1)
    send_length = jnp.sum(chosen * pick(lengths, dp)[None, :], axis=1)

    def spread(start, length):
        row = jnp.where(slot_ids[None, :] < length[:, None], start[:, None] + slot_ids[None, :], -1)
        return row.reshape(-1)[:, None]

    to_owner = spread(send_start, send_length)
    to_loader = spread(arrive_start, arrive_length)

    def exchange(rows):
        blocks = rows.reshape(loaders, capacity, rows.shape[1])
        return lax.all_to_all(blocks, "dp", split_axis=0, concat_axis=0, tiled=True).reshape(rows.shape)

    depth = key_weight.shape[0] // 2
    half = pick(key_weight.reshape(2, depth, kv), core)
    other_z = swap_zlo(half)

    cosine, sine = rope_tables(position)
    key_grad, message = rope_and_spread(to_loader, cosine, sine, rotated_grad, CHUNKS[0])
    message = spread_rows(to_owner, layer_input, 0, CHUNKS[0], message)
    outgoing = spread_rows(to_owner, layer_input, CHUNKS[0], CHUNKS[1])
    message, other_z = lax.optimization_barrier((message, other_z))
    arrived = [exchange(message)]

    pair = jnp.where(zl == 0, jnp.stack([half, other_z]), jnp.stack([other_z, half]))
    mine = jnp.zeros((4, 2, depth, kv), jnp.bfloat16)
    mine = lax.dynamic_update_index_in_dim(mine, pair, yy, 0)
    for n in (1, 3, 2):
        mine = lax.dynamic_update_index_in_dim(mine, along_y(pair, n), (yy - n) % 4, 0)
    mine = mine.reshape(8, depth, kv)
    other = along_core(mine)

    arrived[0], outgoing, later_input, mine, other = lax.optimization_barrier(
        (arrived[0], outgoing, layer_input, mine, other)
    )
    arrived.append(exchange(outgoing))
    key_back = arrived[0][:, CHUNKS[0] :]
    key_loader = lax.dot_general(
        (to_owner == row_ids[None, :]).astype(jnp.bfloat16),
        key_back,
        (((0,), (0,)), ((), ())),
        preferred_element_type=jnp.float32,
    ).astype(jnp.bfloat16)

    gain = norm_gain.astype(jnp.float32)[None, :]
    own = later_input.astype(jnp.float32)
    own_rms = lax.rsqrt(jnp.mean(own * own, axis=-1, keepdims=True) + norm_eps)
    normed = (own * own_rms * gain).astype(jnp.bfloat16)
    scale = 1.0 / math.sqrt(tok_rows * loaders * columns)
    term = (
        lax.dot_general(normed, key_loader, (((0,), (0,)), ((), ())), preferred_element_type=jnp.float32)
        * scale
    ).astype(jnp.bfloat16)
    rows = width // (loaders * columns)
    term = term.reshape(8, 2, 8 * rows, kv)
    got = along_core(pick(term, 1 - core, 1))
    part = (pick(term, core, 1).astype(jnp.float32) + got.astype(jnp.float32)).astype(jnp.bfloat16)

    def reduce(part, axis, me, send):
        total = pick(part, me, axis).astype(jnp.float32)
        for n in (1, 3, 2):
            total = total + send(pick(part, (me + n) % 4, axis), n).astype(jnp.float32)
        return total

    part = reduce(part.reshape(8, 4, 2 * rows, kv), 1, yy, along_y).astype(jnp.bfloat16)
    part = part.reshape(2, 4, 2, rows, kv).transpose(0, 2, 1, 3, 4).reshape(4, 4, rows, kv)
    part = reduce(part, 0, zz, along_z).astype(jnp.bfloat16)
    weight_grad = reduce(part, 0, xx, along_x)

    core_id = jnp.reshape(core, (1,)).astype(jnp.int32)
    select = slot[:, None]
    square = jnp.zeros((tok_rows, 128), jnp.float32)
    inner = jnp.zeros((tok_rows, 128), jnp.float32)
    packed, first = None, 0
    for rows_in, part in zip(arrived, CHUNKS):
        packed, square, inner = first_pass(
            core_id, select, rows_in, key_grad, mine, other, gain, square, inner, packed, first, part, width
        )
        first += part
    input_grad = second_pass(core_id, packed, key_grad, mine, other, gain, square, inner)
    return (input_grad, weight_grad)


def solution(mesh):
    return jax.shard_map(
        body,
        mesh=mesh,
        in_specs=(
            P(("dp", "fsdp"), None),
            P(("dp", "fsdp"), None),
            P(),
            P("fsdp", None),
            P("fsdp", None, None),
            P("fsdp", None, None),
            P("fsdp", None, None),
            P("fsdp", None, None),
            P("fsdp", None, None),
        ),
        out_specs=(P(("dp", "fsdp"), None), P(("dp", "fsdp"), None)),
        check_vma=False,
    )
```

```python
import functools
import math

import jax
import jax.numpy as jnp
from jax import lax
from jax.experimental import pallas as pl
from jax.experimental.pallas import tpu as pltpu
from jax.sharding import PartitionSpec as P

HEAD = 128
KV_HEADS = 4
AXES = ("dp", "fsdp")

rope_base = 500000.0
norm_eps = 1e-05


def place(zh, x, c, y, zl):
    return ((((zh % 2) * 4 + x % 4) * 2 + c % 2) * 4 + y % 4) * 2 + zl % 2


def perm(step):
    pairs = []
    for zh in range(2):
        for x in range(4):
            for c in range(2):
                for y in range(4):
                    for zl in range(2):
                        pairs.append((place(zh, x, c, y, zl), place(*step(zh, x, c, y, zl))))
    return pairs


def along_core(v):
    return lax.ppermute(v, AXES, perm(lambda zh, x, c, y, zl: (zh, x, c + 1, y, zl)))


def along_x(v, n):
    return lax.ppermute(v, AXES, perm(lambda zh, x, c, y, zl: (zh, x + n, c, y, zl)))


def along_y(v, n):
    return lax.ppermute(v, AXES, perm(lambda zh, x, c, y, zl: (zh, x, c, y + n, zl)))


def along_z(v, n):
    def step(zh, x, c, y, zl):
        z = (zh * 2 + zl + n) % 4
        return (z // 2, x, c, y, z % 2)

    return lax.ppermute(v, AXES, perm(step))


def swap_zlo(v):
    return lax.ppermute(v, AXES, perm(lambda zh, x, c, y, zl: (zh, x, c, y, zl + 1)))


def pick(v, i, axis=0):
    return lax.dynamic_index_in_dim(v, i, axis, keepdims=False)


def rope_tables(position):
    half_head = HEAD // 2
    exponent = jnp.arange(half_head, dtype=jnp.float32) * (2.0 / HEAD)
    inverse = jnp.power(jnp.float32(rope_base), -exponent)
    angle = position.astype(jnp.float32)[:, None] * jnp.concatenate([inverse, inverse])[None, :]
    sign = jnp.where(jnp.arange(HEAD) < half_head, 1.0, -1.0).astype(jnp.float32)
    return jnp.cos(angle), jnp.sin(angle) * sign[None, :]


def one_hot(select, count):
    lanes = lax.broadcasted_iota(jnp.int32, (select.shape[0], count), 1)
    return (select == lanes).astype(jnp.float32).astype(jnp.bfloat16)


def rope_kernel(select_ref, cos_ref, sin_ref, rotated_ref, key_ref, out_ref):
    cosine, sine = cos_ref[...], sin_ref[...]
    for head in range(KV_HEADS):
        cols = slice(head * HEAD, (head + 1) * HEAD)
        grads = rotated_ref[:, cols].astype(jnp.float32)
        turned = pltpu.roll(grads, HEAD // 2, 1)
        key_ref[:, cols] = (grads * cosine + turned * sine).astype(jnp.bfloat16)
    spread = one_hot(select_ref[...], key_ref.shape[0])
    out_ref[...] = jnp.dot(spread, key_ref[...], preferred_element_type=jnp.float32).astype(jnp.bfloat16)


def rope_and_spread(select, cosine, sine, rotated, beside):
    rows, kv = rotated.shape
    slots = select.shape[0]
    whole = lambda j: (0, 0)
    return pl.pallas_call(
        rope_kernel,
        grid=(1,),
        in_specs=[pl.BlockSpec(v.shape, whole) for v in (select, cosine, sine, rotated)],
        out_specs=[pl.BlockSpec((rows, kv), whole), pl.BlockSpec((slots, kv), lambda j: (0, beside // kv))],
        out_shape=(
            jax.ShapeDtypeStruct((rows, kv), jnp.bfloat16),
            jax.ShapeDtypeStruct((slots, beside + kv), jnp.bfloat16),
        ),
        cost_estimate=pl.CostEstimate(flops=2 * slots * rows * kv, bytes_accessed=4 << 20, transcendentals=0),
        compiler_params=pltpu.CompilerParams(vmem_limit_bytes=58 << 20),
        name="rope_and_spread",
    )(select, cosine, sine, rotated)


BLOCK = 1024


def spread_kernel(select_ref, rows_ref, *rest):
    out_ref, spread = rest[-2:]

    @pl.when(pl.program_id(0) == 0)
    def _():
        spread[...] = one_hot(select_ref[...], spread.shape[1])

    out_ref[...] = jnp.dot(spread[...], rows_ref[...], preferred_element_type=jnp.float32).astype(jnp.bfloat16)


def spread_rows(select, rows, first, width, beside=None):
    slots, count = select.shape[0], rows.shape[0]
    given = [] if beside is None else [beside]
    total = width if beside is None else beside.shape[1]
    return pl.pallas_call(
        spread_kernel,
        grid=(width // BLOCK,),
        in_specs=[
            pl.BlockSpec((slots, 1), lambda j: (0, 0)),
            pl.BlockSpec((count, BLOCK), lambda j: (0, first // BLOCK + j)),
        ]
        + [pl.BlockSpec(memory_space=pl.ANY)] * len(given),
        out_specs=pl.BlockSpec((slots, BLOCK), lambda j: (0, j)),
        out_shape=jax.ShapeDtypeStruct((slots, total), jnp.bfloat16),
        input_output_aliases={2: 0} if given else {},
        scratch_shapes=[pltpu.VMEM((slots, count), jnp.bfloat16)],
        cost_estimate=pl.CostEstimate(
            flops=2 * slots * count * width, bytes_accessed=2 * (slots + count) * width, transcendentals=0
        ),
        compiler_params=pltpu.CompilerParams(vmem_limit_bytes=58 << 20),
        name="spread_rows",
    )(select, rows, *given)


def lane_sums(values):
    total = values[:, :128]
    for k in range(1, values.shape[1] // 128):
        total = total + values[:, k * 128 : (k + 1) * 128]
    return total


def delta_kernel(core_ref, key_ref, mine_ref, other_ref, gain_ref, out_ref):
    depth = mine_ref.shape[1]
    core = core_ref[0]
    for half, weight_ref in ((core, mine_ref), (1 - core, other_ref)):
        cols = pl.ds(pl.multiple_of(half * depth, depth), depth)
        delta = lax.dot_general(
            key_ref[...], weight_ref[0], (((1,), (1,)), ((), ())), preferred_element_type=jnp.float32
        )
        out_ref[:, cols] = delta * gain_ref[:, cols]


def scaled_delta(core, key_grad, mine, other, gain):
    rows, kv = key_grad.shape
    count, depth = mine.shape[0], mine.shape[1]
    width = gain.shape[1]
    return pl.pallas_call(
        delta_kernel,
        grid_spec=pltpu.PrefetchScalarGridSpec(
            num_scalar_prefetch=1,
            grid=(count,),
            in_specs=[
                pl.BlockSpec((rows, kv), lambda j, core: (0, 0)),
                pl.BlockSpec((1, depth, kv), lambda j, core: (j, 0, 0)),
                pl.BlockSpec((1, depth, kv), lambda j, core: (j, 0, 0)),
                pl.BlockSpec((1, 2 * depth), lambda j, core: (0, j)),
            ],
            out_specs=pl.BlockSpec((rows, 2 * depth), lambda j, core: (0, j)),
        ),
        out_shape=jax.ShapeDtypeStruct((rows, width), jnp.float32),
        cost_estimate=pl.CostEstimate(
            flops=2 * rows * kv * width, bytes_accessed=(4 * rows + 2 * kv) * width, transcendentals=0
        ),
        compiler_params=pltpu.CompilerParams(vmem_limit_bytes=58 << 20),
        name="scaled_delta",
    )(core, key_grad, mine, other, gain)


def place_and_sum(gather, arrived_ref, scaled_ref, square_ref, inner_ref):
    values = jnp.dot(gather[...], arrived_ref[...], preferred_element_type=jnp.float32)
    square_ref[...] += lane_sums(values * values)
    inner_ref[...] += lane_sums(scaled_ref[...] * values)
    return values.astype(jnp.bfloat16)


def first_pass_kernel(select_ref, arrived_ref, scaled_ref, square_in, inner_in, *rest):
    packed_ref, square_ref, inner_ref, gather = rest[-4:]

    @pl.when(pl.program_id(0) == 0)
    def _():
        gather[...] = one_hot(select_ref[...], gather.shape[1])
        square_ref[...] = square_in[...]
        inner_ref[...] = inner_in[...]

    packed_ref[...] = place_and_sum(gather, arrived_ref, scaled_ref, square_ref, inner_ref)


def first_pass(select, arrived, scaled, square, inner, packed, first, part, total):
    rows, slots = select.shape[0], arrived.shape[0]
    base = first // BLOCK
    whole = lambda j: (0, 0)
    column = lambda j: (0, base + j)
    sums = jax.ShapeDtypeStruct((rows, 128), jnp.float32)
    operands = [select, arrived, scaled, square, inner]
    in_specs = [
        pl.BlockSpec((rows, 1), whole),
        pl.BlockSpec((slots, BLOCK), lambda j: (0, j)),
        pl.BlockSpec((rows, BLOCK), column),
        pl.BlockSpec((rows, 128), whole),
        pl.BlockSpec((rows, 128), whole),
    ]
    aliases = {}
    if packed is not None:
        aliases = {len(operands): 0}
        operands.append(packed)
        in_specs.append(pl.BlockSpec(memory_space=pl.ANY))
    return pl.pallas_call(
        first_pass_kernel,
        grid=(part // BLOCK,),
        in_specs=in_specs,
        out_specs=[
            pl.BlockSpec((rows, BLOCK), column),
            pl.BlockSpec((rows, 128), whole),
            pl.BlockSpec((rows, 128), whole),
        ],
        scratch_shapes=[pltpu.VMEM((rows, slots), jnp.bfloat16)],
        out_shape=(jax.ShapeDtypeStruct((rows, total), jnp.bfloat16), sums, sums),
        input_output_aliases=aliases,
        cost_estimate=pl.CostEstimate(
            flops=2 * rows * slots * part, bytes_accessed=(2 * slots + 6 * rows) * part, transcendentals=0
        ),
        compiler_params=pltpu.CompilerParams(vmem_limit_bytes=58 << 20),
        name="first_pass",
    )(*operands)


def last_pass_kernel(
    select_ref, arrived_ref, scaled_ref, packed_ref, square_in, inner_in,
    out_ref, gather, square, inner, inv, coef, kept, kept_scaled, *, early, late, width,
):
    step = pl.program_id(0)

    @pl.when(step == 0)
    def _():
        gather[...] = one_hot(select_ref[...], gather.shape[1])
        square[...] = square_in[...]
        inner[...] = inner_in[...]

    @pl.when(step < late)
    def _():
        kept[step] = place_and_sum(gather, arrived_ref, scaled_ref, square, inner)
        kept_scaled[step] = scaled_ref[...]

    @pl.when(step == late)
    def _():
        inverse = lax.rsqrt(jnp.sum(square[...], axis=1, keepdims=True) * (1.0 / width) + norm_eps)
        inv[...] = inverse
        coef[...] = inverse * inverse * (jnp.sum(inner[...], axis=1, keepdims=True) * (1.0 / width))

    def finish(scaled, values):
        out_ref[...] = (inv[...] * (scaled - values.astype(jnp.float32) * coef[...])).astype(jnp.bfloat16)

    @pl.when((step >= late) & (step < late + early))
    def _():
        finish(scaled_ref[...], packed_ref[...])

    @pl.when(step >= late + early)
    def _():
        i = step - (late + early)
        finish(kept_scaled[i], kept[i])


def last_pass(select, arrived, scaled, packed, square, inner):
    rows, width = scaled.shape
    slots = arrived.shape[0]
    early, late = packed.shape[1] // BLOCK, arrived.shape[1] // BLOCK
    whole = lambda j: (0, 0)
    return pl.pallas_call(
        functools.partial(last_pass_kernel, early=early, late=late, width=width),
        grid=(2 * late + early,),
        in_specs=[
            pl.BlockSpec((rows, 1), whole),
            pl.BlockSpec((slots, BLOCK), lambda j: (0, jnp.minimum(j, late - 1))),
            pl.BlockSpec(
                (rows, BLOCK), lambda j: (0, jnp.where(j < late, early + j, jnp.minimum(j - late, early - 1)))
            ),
            pl.BlockSpec((rows, BLOCK), lambda j: (0, jnp.clip(j - late, 0, early - 1))),
            pl.BlockSpec((rows, 128), whole),
            pl.BlockSpec((rows, 128), whole),
        ],
        out_specs=pl.BlockSpec((rows, BLOCK), lambda j: (0, jnp.maximum(j - late, 0))),
        scratch_shapes=[
            pltpu.VMEM((rows, slots), jnp.bfloat16),
            pltpu.VMEM((rows, 128), jnp.float32),
            pltpu.VMEM((rows, 128), jnp.float32),
            pltpu.VMEM((rows, 1), jnp.float32),
            pltpu.VMEM((rows, 1), jnp.float32),
            pltpu.VMEM((late, rows, BLOCK), jnp.bfloat16),
            pltpu.VMEM((late, rows, BLOCK), jnp.float32),
        ],
        out_shape=jax.ShapeDtypeStruct((rows, width), jnp.bfloat16),
        cost_estimate=pl.CostEstimate(
            flops=2 * rows * slots * late * BLOCK, bytes_accessed=24 << 20, transcendentals=0
        ),
        compiler_params=pltpu.CompilerParams(vmem_limit_bytes=58 << 20),
        name="last_pass",
    )(select, arrived, scaled, packed, square, inner)


CHUNKS = (3072, 5120)


def body(
    layer_input,
    rotated_grad,
    norm_gain,
    key_weight,
    block_length,
    block_owner,
    block_source_offset,
    block_pack_offset,
    block_position,
):
    tok_rows, width = layer_input.shape
    kv = rotated_grad.shape[1]
    loaders = lax.axis_size("dp")
    columns = lax.axis_size("fsdp")
    dp = lax.axis_index("dp")
    fs = lax.axis_index("fsdp")
    zh, xx, core = dp // 8, (dp // 2) % 4, dp % 2
    yy, zl = fs // 2, fs % 2
    zz = zh * 2 + zl
    capacity = 2 * tok_rows // loaders
    lengths = block_length[0]
    owners = block_owner[0]
    source_offsets = block_source_offset[0]
    pack_offsets = block_pack_offset[0]
    positions = block_position[0]
    shard_ids = jnp.arange(loaders, dtype=jnp.int32)
    slot_ids = jnp.arange(capacity, dtype=jnp.int32)
    row_ids = jnp.arange(tok_rows, dtype=jnp.int32)

    mine = (owners == dp).astype(jnp.int32)
    arrive_start = jnp.sum(mine * pack_offsets, axis=1)
    arrive_length = jnp.sum(mine * lengths, axis=1)
    arrive_position = jnp.sum(mine * positions, axis=1)
    inside = (
        (row_ids[:, None] >= arrive_start[None, :])
        & (row_ids[:, None] < (arrive_start + arrive_length)[None, :])
    ).astype(jnp.int32)
    position = row_ids + jnp.sum(inside * (arrive_position - arrive_start)[None, :], axis=1)
    slot = row_ids + jnp.sum(inside * (shard_ids * capacity - arrive_start)[None, :], axis=1)

    chosen = (pick(owners, dp)[None, :] == shard_ids[:, None]).astype(jnp.int32)
    send_start = jnp.sum(chosen * pick(source_offsets, dp)[None, :], axis=1)
    send_length = jnp.sum(chosen * pick(lengths, dp)[None, :], axis=1)

    def spread(start, length):
        row = jnp.where(slot_ids[None, :] < length[:, None], start[:, None] + slot_ids[None, :], -1)
        return row.reshape(-1)[:, None]

    to_owner = spread(send_start, send_length)
    to_loader = spread(arrive_start, arrive_length)

    def exchange(rows):
        blocks = rows.reshape(loaders, capacity, rows.shape[1])
        return lax.all_to_all(blocks, "dp", split_axis=0, concat_axis=0, tiled=True).reshape(rows.shape)

    depth = key_weight.shape[0] // 2
    half = pick(key_weight.reshape(2, depth, kv), core)
    other_z = swap_zlo(half)

    cosine, sine = rope_tables(position)
    key_grad, message = rope_and_spread(to_loader, cosine, sine, rotated_grad, CHUNKS[0])
    message = spread_rows(to_owner, layer_input, 0, CHUNKS[0], message)
    outgoing = [
        spread_rows(to_owner, layer_input, sum(CHUNKS[:i]), CHUNKS[i]) for i in range(1, len(CHUNKS))
    ]
    message, other_z = lax.optimization_barrier((message, other_z))
    arrived = [exchange(message)]

    pair = jnp.where(zl == 0, jnp.stack([half, other_z]), jnp.stack([other_z, half]))
    mine = jnp.zeros((4, 2, depth, kv), jnp.bfloat16)
    mine = lax.dynamic_update_index_in_dim(mine, pair, yy, 0)
    for n in (1, 3, 2):
        mine = lax.dynamic_update_index_in_dim(mine, along_y(pair, n), (yy - n) % 4, 0)
    mine = mine.reshape(8, depth, kv)
    other = along_core(mine)

    first_in, outgoing[0], later_input, mine, other = lax.optimization_barrier(
        (arrived[0], outgoing[0], layer_input, mine, other)
    )
    arrived[0] = first_in
    for rows_out in outgoing:
        arrived.append(exchange(rows_out))
    key_back = arrived[0][:, CHUNKS[0] :]
    key_loader = lax.dot_general(
        (to_owner == row_ids[None, :]).astype(jnp.bfloat16),
        key_back,
        (((0,), (0,)), ((), ())),
        preferred_element_type=jnp.float32,
    ).astype(jnp.bfloat16)

    gain = norm_gain.astype(jnp.float32)[None, :]
    own = later_input.astype(jnp.float32)
    own_rms = lax.rsqrt(jnp.mean(own * own, axis=-1, keepdims=True) + norm_eps)
    normed = (own * own_rms * gain).astype(jnp.bfloat16)
    scale = 1.0 / math.sqrt(tok_rows * loaders * columns)
    term = (
        lax.dot_general(normed, key_loader, (((0,), (0,)), ((), ())), preferred_element_type=jnp.float32)
        * scale
    ).astype(jnp.bfloat16)
    rows = width // (loaders * columns)
    term = term.reshape(8, 2, 8 * rows, kv)
    got = along_core(pick(term, 1 - core, 1))
    part = (pick(term, core, 1).astype(jnp.float32) + got.astype(jnp.float32)).astype(jnp.bfloat16)

    def reduce(part, axis, me, send):
        total = pick(part, me, axis).astype(jnp.float32)
        for n in (1, 3, 2):
            total = total + send(pick(part, (me + n) % 4, axis), n).astype(jnp.float32)
        return total

    part = reduce(part.reshape(8, 4, 2 * rows, kv), 1, yy, along_y).astype(jnp.bfloat16)
    core_id = jnp.reshape(core, (1,)).astype(jnp.int32)
    select = slot[:, None]
    square = jnp.zeros((tok_rows, 128), jnp.float32)
    inner = jnp.zeros((tok_rows, 128), jnp.float32)
    scaled = scaled_delta(core_id, key_grad, mine, other, gain)
    packed, first = None, 0
    for rows_in, size in zip(arrived[:-1], CHUNKS[:-1]):
        packed, square, inner = first_pass(
            select, rows_in, scaled, square, inner, packed, first, size, sum(CHUNKS[:-1])
        )
        first += size
    part, square, inner = lax.optimization_barrier((part, square, inner))
    part = part.reshape(2, 4, 2, rows, kv).transpose(0, 2, 1, 3, 4).reshape(4, 4, rows, kv)
    part = reduce(part, 0, zz, along_z).astype(jnp.bfloat16)
    weight_grad = reduce(part, 0, xx, along_x)

    input_grad = last_pass(select, arrived[-1], scaled, packed, square, inner)
    return (input_grad, weight_grad)


def solution(mesh):
    return jax.shard_map(
        body,
        mesh=mesh,
        in_specs=(
            P(("dp", "fsdp"), None),
            P(("dp", "fsdp"), None),
            P(),
            P("fsdp", None),
            P("fsdp", None, None),
            P("fsdp", None, None),
            P("fsdp", None, None),
            P("fsdp", None, None),
            P("fsdp", None, None),
        ),
        out_specs=(P(("dp", "fsdp"), None), P(("dp", "fsdp"), None)),
        check_vma=False,
    )
```

```python
import functools
import math

import jax
import jax.numpy as jnp
from jax import lax
from jax.experimental import pallas as pl
from jax.experimental.pallas import tpu as pltpu
from jax.sharding import PartitionSpec as P

HEAD = 128
KV_HEADS = 4
AXES = ("dp", "fsdp")

rope_base = 500000.0
norm_eps = 1e-05


def place(zh, x, c, y, zl):
    return ((((zh % 2) * 4 + x % 4) * 2 + c % 2) * 4 + y % 4) * 2 + zl % 2


def perm(step):
    pairs = []
    for zh in range(2):
        for x in range(4):
            for c in range(2):
                for y in range(4):
                    for zl in range(2):
                        pairs.append((place(zh, x, c, y, zl), place(*step(zh, x, c, y, zl))))
    return pairs


def along_core(v):
    return lax.ppermute(v, AXES, perm(lambda zh, x, c, y, zl: (zh, x, c + 1, y, zl)))


def along_x(v, n):
    return lax.ppermute(v, AXES, perm(lambda zh, x, c, y, zl: (zh, x + n, c, y, zl)))


def along_y(v, n):
    return lax.ppermute(v, AXES, perm(lambda zh, x, c, y, zl: (zh, x, c, y + n, zl)))


def along_z(v, n):
    def step(zh, x, c, y, zl):
        z = (zh * 2 + zl + n) % 4
        return (z // 2, x, c, y, z % 2)

    return lax.ppermute(v, AXES, perm(step))


def swap_zlo(v):
    return lax.ppermute(v, AXES, perm(lambda zh, x, c, y, zl: (zh, x, c, y, zl + 1)))


def pick(v, i, axis=0):
    return lax.dynamic_index_in_dim(v, i, axis, keepdims=False)


def rope_tables(position):
    half_head = HEAD // 2
    exponent = jnp.arange(half_head, dtype=jnp.float32) * (2.0 / HEAD)
    inverse = jnp.power(jnp.float32(rope_base), -exponent)
    angle = position.astype(jnp.float32)[:, None] * jnp.concatenate([inverse, inverse])[None, :]
    sign = jnp.where(jnp.arange(HEAD) < half_head, 1.0, -1.0).astype(jnp.float32)
    return jnp.cos(angle), jnp.sin(angle) * sign[None, :]


def one_hot(select, count):
    lanes = lax.broadcasted_iota(jnp.int32, (select.shape[0], count), 1)
    return (select == lanes).astype(jnp.float32).astype(jnp.bfloat16)


def rope_kernel(select_ref, cos_ref, sin_ref, rotated_ref, key_ref, out_ref):
    cosine, sine = cos_ref[...], sin_ref[...]
    for head in range(KV_HEADS):
        cols = slice(head * HEAD, (head + 1) * HEAD)
        grads = rotated_ref[:, cols].astype(jnp.float32)
        turned = pltpu.roll(grads, HEAD // 2, 1)
        key_ref[:, cols] = (grads * cosine + turned * sine).astype(jnp.bfloat16)
    spread = one_hot(select_ref[...], key_ref.shape[0])
    out_ref[...] = jnp.dot(spread, key_ref[...], preferred_element_type=jnp.float32).astype(jnp.bfloat16)


def rope_and_spread(select, cosine, sine, rotated, beside):
    rows, kv = rotated.shape
    slots = select.shape[0]
    whole = lambda j: (0, 0)
    return pl.pallas_call(
        rope_kernel,
        grid=(1,),
        in_specs=[pl.BlockSpec(v.shape, whole) for v in (select, cosine, sine, rotated)],
        out_specs=[pl.BlockSpec((rows, kv), whole), pl.BlockSpec((slots, kv), lambda j: (0, beside // kv))],
        out_shape=(
            jax.ShapeDtypeStruct((rows, kv), jnp.bfloat16),
            jax.ShapeDtypeStruct((slots, beside + kv), jnp.bfloat16),
        ),
        cost_estimate=pl.CostEstimate(flops=2 * slots * rows * kv, bytes_accessed=4 << 20, transcendentals=0),
        compiler_params=pltpu.CompilerParams(vmem_limit_bytes=58 << 20),
        name="rope_and_spread",
    )(select, cosine, sine, rotated)


BLOCK = 1024


def spread_kernel(select_ref, rows_ref, *rest):
    out_ref, spread = rest[-2:]

    @pl.when(pl.program_id(0) == 0)
    def _():
        spread[...] = one_hot(select_ref[...], spread.shape[1])

    out_ref[...] = jnp.dot(spread[...], rows_ref[...], preferred_element_type=jnp.float32).astype(jnp.bfloat16)


def spread_rows(select, rows, first, width, beside=None):
    slots, count = select.shape[0], rows.shape[0]
    given = [] if beside is None else [beside]
    total = width if beside is None else beside.shape[1]
    return pl.pallas_call(
        spread_kernel,
        grid=(width // BLOCK,),
        in_specs=[
            pl.BlockSpec((slots, 1), lambda j: (0, 0)),
            pl.BlockSpec((count, BLOCK), lambda j: (0, first // BLOCK + j)),
        ]
        + [pl.BlockSpec(memory_space=pl.ANY)] * len(given),
        out_specs=pl.BlockSpec((slots, BLOCK), lambda j: (0, j)),
        out_shape=jax.ShapeDtypeStruct((slots, total), jnp.bfloat16),
        input_output_aliases={2: 0} if given else {},
        scratch_shapes=[pltpu.VMEM((slots, count), jnp.bfloat16)],
        cost_estimate=pl.CostEstimate(
            flops=2 * slots * count * width, bytes_accessed=2 * (slots + count) * width, transcendentals=0
        ),
        compiler_params=pltpu.CompilerParams(vmem_limit_bytes=58 << 20),
        name="spread_rows",
    )(select, rows, *given)


def lane_sums(values):
    total = values[:, :128]
    for k in range(1, values.shape[1] // 128):
        total = total + values[:, k * 128 : (k + 1) * 128]
    return total


def delta_kernel(core_ref, key_ref, mine_ref, other_ref, gain_ref, out_ref):
    depth = mine_ref.shape[1]
    core = core_ref[0]
    for half, weight_ref in ((core, mine_ref), (1 - core, other_ref)):
        cols = pl.ds(pl.multiple_of(half * depth, depth), depth)
        delta = lax.dot_general(
            key_ref[...], weight_ref[0], (((1,), (1,)), ((), ())), preferred_element_type=jnp.float32
        )
        out_ref[:, cols] = (delta * gain_ref[:, cols]).astype(jnp.bfloat16)


def scaled_delta(core, key_grad, mine, other, gain):
    rows, kv = key_grad.shape
    count, depth = mine.shape[0], mine.shape[1]
    width = gain.shape[1]
    return pl.pallas_call(
        delta_kernel,
        grid_spec=pltpu.PrefetchScalarGridSpec(
            num_scalar_prefetch=1,
            grid=(count,),
            in_specs=[
                pl.BlockSpec((rows, kv), lambda j, core: (0, 0)),
                pl.BlockSpec((1, depth, kv), lambda j, core: (j, 0, 0)),
                pl.BlockSpec((1, depth, kv), lambda j, core: (j, 0, 0)),
                pl.BlockSpec((1, 2 * depth), lambda j, core: (0, j)),
            ],
            out_specs=pl.BlockSpec((rows, 2 * depth), lambda j, core: (0, j)),
        ),
        out_shape=jax.ShapeDtypeStruct((rows, width), jnp.bfloat16),
        cost_estimate=pl.CostEstimate(
            flops=2 * rows * kv * width, bytes_accessed=2 * (rows + kv) * width, transcendentals=0
        ),
        compiler_params=pltpu.CompilerParams(vmem_limit_bytes=58 << 20),
        name="scaled_delta",
    )(core, key_grad, mine, other, gain)


def place_and_sum(gather, arrived_ref, scaled_ref, square_ref, inner_ref):
    values = jnp.dot(gather[...], arrived_ref[...], preferred_element_type=jnp.float32)
    square_ref[...] += lane_sums(values * values)
    inner_ref[...] += lane_sums(scaled_ref[...].astype(jnp.float32) * values)
    return values.astype(jnp.bfloat16)


def first_pass_kernel(select_ref, arrived_ref, scaled_ref, square_in, inner_in, *rest):
    packed_ref, square_ref, inner_ref, gather = rest[-4:]

    @pl.when(pl.program_id(0) == 0)
    def _():
        gather[...] = one_hot(select_ref[...], gather.shape[1])
        square_ref[...] = square_in[...]
        inner_ref[...] = inner_in[...]

    packed_ref[...] = place_and_sum(gather, arrived_ref, scaled_ref, square_ref, inner_ref)


def first_pass(select, arrived, scaled, square, inner, packed, first, part, total):
    rows, slots = select.shape[0], arrived.shape[0]
    base = first // BLOCK
    whole = lambda j: (0, 0)
    column = lambda j: (0, base + j)
    sums = jax.ShapeDtypeStruct((rows, 128), jnp.float32)
    operands = [select, arrived, scaled, square, inner]
    in_specs = [
        pl.BlockSpec((rows, 1), whole),
        pl.BlockSpec((slots, BLOCK), lambda j: (0, j)),
        pl.BlockSpec((rows, BLOCK), column),
        pl.BlockSpec((rows, 128), whole),
        pl.BlockSpec((rows, 128), whole),
    ]
    aliases = {}
    if packed is not None:
        aliases = {len(operands): 0}
        operands.append(packed)
        in_specs.append(pl.BlockSpec(memory_space=pl.ANY))
    return pl.pallas_call(
        first_pass_kernel,
        grid=(part // BLOCK,),
        in_specs=in_specs,
        out_specs=[
            pl.BlockSpec((rows, BLOCK), column),
            pl.BlockSpec((rows, 128), whole),
            pl.BlockSpec((rows, 128), whole),
        ],
        scratch_shapes=[pltpu.VMEM((rows, slots), jnp.bfloat16)],
        out_shape=(jax.ShapeDtypeStruct((rows, total), jnp.bfloat16), sums, sums),
        input_output_aliases=aliases,
        cost_estimate=pl.CostEstimate(
            flops=2 * rows * slots * part, bytes_accessed=(2 * slots + 6 * rows) * part, transcendentals=0
        ),
        compiler_params=pltpu.CompilerParams(vmem_limit_bytes=58 << 20),
        name="first_pass",
    )(*operands)


def last_pass_kernel(
    select_ref, arrived_ref, scaled_ref, packed_ref, square_in, inner_in,
    out_ref, gather, square, inner, inv, coef, kept, kept_scaled, *, early, late, width,
):
    step = pl.program_id(0)

    @pl.when(step == 0)
    def _():
        gather[...] = one_hot(select_ref[...], gather.shape[1])
        square[...] = square_in[...]
        inner[...] = inner_in[...]

    @pl.when(step < late)
    def _():
        kept[step] = place_and_sum(gather, arrived_ref, scaled_ref, square, inner)
        kept_scaled[step] = scaled_ref[...]

    @pl.when(step == late)
    def _():
        inverse = lax.rsqrt(jnp.sum(square[...], axis=1, keepdims=True) * (1.0 / width) + norm_eps)
        inv[...] = inverse
        coef[...] = inverse * inverse * (jnp.sum(inner[...], axis=1, keepdims=True) * (1.0 / width))

    def finish(scaled, values):
        out_ref[...] = (
            inv[...] * (scaled.astype(jnp.float32) - values.astype(jnp.float32) * coef[...])
        ).astype(jnp.bfloat16)

    @pl.when((step >= late) & (step < late + early))
    def _():
        finish(scaled_ref[...], packed_ref[...])

    @pl.when(step >= late + early)
    def _():
        i = step - (late + early)
        finish(kept_scaled[i], kept[i])


def last_pass(select, arrived, scaled, packed, square, inner):
    rows, width = scaled.shape
    slots = arrived.shape[0]
    early, late = packed.shape[1] // BLOCK, arrived.shape[1] // BLOCK
    whole = lambda j: (0, 0)
    return pl.pallas_call(
        functools.partial(last_pass_kernel, early=early, late=late, width=width),
        grid=(2 * late + early,),
        in_specs=[
            pl.BlockSpec((rows, 1), whole),
            pl.BlockSpec((slots, BLOCK), lambda j: (0, jnp.minimum(j, late - 1))),
            pl.BlockSpec(
                (rows, BLOCK), lambda j: (0, jnp.where(j < late, early + j, jnp.minimum(j - late, early - 1)))
            ),
            pl.BlockSpec((rows, BLOCK), lambda j: (0, jnp.clip(j - late, 0, early - 1))),
            pl.BlockSpec((rows, 128), whole),
            pl.BlockSpec((rows, 128), whole),
        ],
        out_specs=pl.BlockSpec((rows, BLOCK), lambda j: (0, jnp.maximum(j - late, 0))),
        scratch_shapes=[
            pltpu.VMEM((rows, slots), jnp.bfloat16),
            pltpu.VMEM((rows, 128), jnp.float32),
            pltpu.VMEM((rows, 128), jnp.float32),
            pltpu.VMEM((rows, 1), jnp.float32),
            pltpu.VMEM((rows, 1), jnp.float32),
            pltpu.VMEM((late, rows, BLOCK), jnp.bfloat16),
            pltpu.VMEM((late, rows, BLOCK), jnp.bfloat16),
        ],
        out_shape=jax.ShapeDtypeStruct((rows, width), jnp.bfloat16),
        cost_estimate=pl.CostEstimate(
            flops=2 * rows * slots * late * BLOCK, bytes_accessed=24 << 20, transcendentals=0
        ),
        compiler_params=pltpu.CompilerParams(vmem_limit_bytes=58 << 20),
        name="last_pass",
    )(select, arrived, scaled, packed, square, inner)


CHUNKS = (3072, 5120)


def body(
    layer_input,
    rotated_grad,
    norm_gain,
    key_weight,
    block_length,
    block_owner,
    block_source_offset,
    block_pack_offset,
    block_position,
):
    tok_rows, width = layer_input.shape
    kv = rotated_grad.shape[1]
    loaders = lax.axis_size("dp")
    columns = lax.axis_size("fsdp")
    dp = lax.axis_index("dp")
    fs = lax.axis_index("fsdp")
    zh, xx, core = dp // 8, (dp // 2) % 4, dp % 2
    yy, zl = fs // 2, fs % 2
    zz = zh * 2 + zl
    capacity = 2 * tok_rows // loaders
    lengths = block_length[0]
    owners = block_owner[0]
    source_offsets = block_source_offset[0]
    pack_offsets = block_pack_offset[0]
    positions = block_position[0]
    shard_ids = jnp.arange(loaders, dtype=jnp.int32)
    slot_ids = jnp.arange(capacity, dtype=jnp.int32)
    row_ids = jnp.arange(tok_rows, dtype=jnp.int32)

    mine = (owners == dp).astype(jnp.int32)
    arrive_start = jnp.sum(mine * pack_offsets, axis=1)
    arrive_length = jnp.sum(mine * lengths, axis=1)
    arrive_position = jnp.sum(mine * positions, axis=1)
    inside = (
        (row_ids[:, None] >= arrive_start[None, :])
        & (row_ids[:, None] < (arrive_start + arrive_length)[None, :])
    ).astype(jnp.int32)
    position = row_ids + jnp.sum(inside * (arrive_position - arrive_start)[None, :], axis=1)
    slot = row_ids + jnp.sum(inside * (shard_ids * capacity - arrive_start)[None, :], axis=1)

    chosen = (pick(owners, dp)[None, :] == shard_ids[:, None]).astype(jnp.int32)
    send_start = jnp.sum(chosen * pick(source_offsets, dp)[None, :], axis=1)
    send_length = jnp.sum(chosen * pick(lengths, dp)[None, :], axis=1)

    def spread(start, length):
        row = jnp.where(slot_ids[None, :] < length[:, None], start[:, None] + slot_ids[None, :], -1)
        return row.reshape(-1)[:, None]

    to_owner = spread(send_start, send_length)
    to_loader = spread(arrive_start, arrive_length)

    def exchange(rows):
        blocks = rows.reshape(loaders, capacity, rows.shape[1])
        return lax.all_to_all(blocks, "dp", split_axis=0, concat_axis=0, tiled=True).reshape(rows.shape)

    depth = key_weight.shape[0] // 2
    half = pick(key_weight.reshape(2, depth, kv), core)
    other_z = swap_zlo(half)

    cosine, sine = rope_tables(position)
    key_grad, message = rope_and_spread(to_loader, cosine, sine, rotated_grad, CHUNKS[0])
    message = spread_rows(to_owner, layer_input, 0, CHUNKS[0], message)
    outgoing = [
        spread_rows(to_owner, layer_input, sum(CHUNKS[:i]), CHUNKS[i]) for i in range(1, len(CHUNKS))
    ]
    message, other_z = lax.optimization_barrier((message, other_z))
    arrived = [exchange(message)]

    pair = jnp.where(zl == 0, jnp.stack([half, other_z]), jnp.stack([other_z, half]))
    mine = jnp.zeros((4, 2, depth, kv), jnp.bfloat16)
    mine = lax.dynamic_update_index_in_dim(mine, pair, yy, 0)
    for n in (1, 3, 2):
        mine = lax.dynamic_update_index_in_dim(mine, along_y(pair, n), (yy - n) % 4, 0)
    mine = mine.reshape(8, depth, kv)
    other = along_core(mine)

    first_in, outgoing[0], later_input, mine, other = lax.optimization_barrier(
        (arrived[0], outgoing[0], layer_input, mine, other)
    )
    arrived[0] = first_in
    for rows_out in outgoing:
        arrived.append(exchange(rows_out))
    key_back = arrived[0][:, CHUNKS[0] :]
    key_loader = lax.dot_general(
        (to_owner == row_ids[None, :]).astype(jnp.bfloat16),
        key_back,
        (((0,), (0,)), ((), ())),
        preferred_element_type=jnp.float32,
    ).astype(jnp.bfloat16)

    gain = norm_gain.astype(jnp.float32)[None, :]
    own = later_input.astype(jnp.float32)
    own_rms = lax.rsqrt(jnp.mean(own * own, axis=-1, keepdims=True) + norm_eps)
    normed = (own * own_rms * gain).astype(jnp.bfloat16)
    scale = 1.0 / math.sqrt(tok_rows * loaders * columns)
    term = (
        lax.dot_general(normed, key_loader, (((0,), (0,)), ((), ())), preferred_element_type=jnp.float32)
        * scale
    ).astype(jnp.bfloat16)
    rows = width // (loaders * columns)
    term = term.reshape(8, 2, 8 * rows, kv)
    got = along_core(pick(term, 1 - core, 1))
    part = (pick(term, core, 1).astype(jnp.float32) + got.astype(jnp.float32)).astype(jnp.bfloat16)

    def reduce(part, axis, me, send):
        total = pick(part, me, axis).astype(jnp.float32)
        for n in (1, 3, 2):
            total = total + send(pick(part, (me + n) % 4, axis), n).astype(jnp.float32)
        return total

    part = reduce(part.reshape(8, 4, 2 * rows, kv), 1, yy, along_y).astype(jnp.bfloat16)
    core_id = jnp.reshape(core, (1,)).astype(jnp.int32)
    select = slot[:, None]
    square = jnp.zeros((tok_rows, 128), jnp.float32)
    inner = jnp.zeros((tok_rows, 128), jnp.float32)
    scaled = scaled_delta(core_id, key_grad, mine, other, gain)
    packed, first = None, 0
    for rows_in, size in zip(arrived[:-1], CHUNKS[:-1]):
        packed, square, inner = first_pass(
            select, rows_in, scaled, square, inner, packed, first, size, sum(CHUNKS[:-1])
        )
        first += size
    part, square, inner = lax.optimization_barrier((part, square, inner))
    part = part.reshape(2, 4, 2, rows, kv).transpose(0, 2, 1, 3, 4).reshape(4, 4, rows, kv)
    part = reduce(part, 0, zz, along_z).astype(jnp.bfloat16)
    kept = pick(part, xx)
    pieces = [along_x(pick(part, (xx + n) % 4), n) for n in (1, 3, 2)]

    input_grad = last_pass(select, arrived[-1], scaled, packed, square, inner)
    input_grad, kept, pieces = lax.optimization_barrier((input_grad, kept, pieces))
    weight_grad = kept.astype(jnp.float32)
    for piece in pieces:
        weight_grad = weight_grad + piece.astype(jnp.float32)
    return (input_grad, weight_grad)


def solution(mesh):
    return jax.shard_map(
        body,
        mesh=mesh,
        in_specs=(
            P(("dp", "fsdp"), None),
            P(("dp", "fsdp"), None),
            P(),
            P("fsdp", None),
            P("fsdp", None, None),
            P("fsdp", None, None),
            P("fsdp", None, None),
            P("fsdp", None, None),
            P("fsdp", None, None),
        ),
        out_specs=(P(("dp", "fsdp"), None), P(("dp", "fsdp"), None)),
        check_vma=False,
    )
```

```python
import functools
import math

import jax
import jax.numpy as jnp
from jax import lax
from jax.experimental import pallas as pl
from jax.experimental.pallas import tpu as pltpu
from jax.sharding import PartitionSpec as P

HEAD = 128
KV_HEADS = 4
AXES = ("dp", "fsdp")

rope_base = 500000.0
norm_eps = 1e-05


def place(zh, x, c, y, zl):
    return ((((zh % 2) * 4 + x % 4) * 2 + c % 2) * 4 + y % 4) * 2 + zl % 2


def perm(step):
    pairs = []
    for zh in range(2):
        for x in range(4):
            for c in range(2):
                for y in range(4):
                    for zl in range(2):
                        pairs.append((place(zh, x, c, y, zl), place(*step(zh, x, c, y, zl))))
    return pairs


def along_core(v):
    return lax.ppermute(v, AXES, perm(lambda zh, x, c, y, zl: (zh, x, c + 1, y, zl)))


def along_x(v, n):
    return lax.ppermute(v, AXES, perm(lambda zh, x, c, y, zl: (zh, x + n, c, y, zl)))


def along_y(v, n):
    return lax.ppermute(v, AXES, perm(lambda zh, x, c, y, zl: (zh, x, c, y + n, zl)))


def along_z(v, n):
    def step(zh, x, c, y, zl):
        z = (zh * 2 + zl + n) % 4
        return (z // 2, x, c, y, z % 2)

    return lax.ppermute(v, AXES, perm(step))


def swap_zlo(v):
    return lax.ppermute(v, AXES, perm(lambda zh, x, c, y, zl: (zh, x, c, y, zl + 1)))


def pick(v, i, axis=0):
    return lax.dynamic_index_in_dim(v, i, axis, keepdims=False)


def rope_tables(position):
    half_head = HEAD // 2
    exponent = jnp.arange(half_head, dtype=jnp.float32) * (2.0 / HEAD)
    inverse = jnp.power(jnp.float32(rope_base), -exponent)
    angle = position.astype(jnp.float32)[:, None] * jnp.concatenate([inverse, inverse])[None, :]
    sign = jnp.where(jnp.arange(HEAD) < half_head, 1.0, -1.0).astype(jnp.float32)
    return jnp.cos(angle), jnp.sin(angle) * sign[None, :]


def one_hot(select, count):
    lanes = lax.broadcasted_iota(jnp.int32, (select.shape[0], count), 1)
    return (select == lanes).astype(jnp.float32).astype(jnp.bfloat16)


def rope_kernel(select_ref, cos_ref, sin_ref, rotated_ref, key_ref, out_ref):
    cosine, sine = cos_ref[...], sin_ref[...]
    for head in range(KV_HEADS):
        cols = slice(head * HEAD, (head + 1) * HEAD)
        grads = rotated_ref[:, cols].astype(jnp.float32)
        turned = pltpu.roll(grads, HEAD // 2, 1)
        key_ref[:, cols] = (grads * cosine + turned * sine).astype(jnp.bfloat16)
    spread = one_hot(select_ref[...], key_ref.shape[0])
    out_ref[...] = jnp.dot(spread, key_ref[...], preferred_element_type=jnp.float32).astype(jnp.bfloat16)


def rope_and_spread(select, cosine, sine, rotated, beside):
    rows, kv = rotated.shape
    slots = select.shape[0]
    whole = lambda j: (0, 0)
    return pl.pallas_call(
        rope_kernel,
        grid=(1,),
        in_specs=[pl.BlockSpec(v.shape, whole) for v in (select, cosine, sine, rotated)],
        out_specs=[pl.BlockSpec((rows, kv), whole), pl.BlockSpec((slots, kv), lambda j: (0, beside // kv))],
        out_shape=(
            jax.ShapeDtypeStruct((rows, kv), jnp.bfloat16),
            jax.ShapeDtypeStruct((slots, beside + kv), jnp.bfloat16),
        ),
        cost_estimate=pl.CostEstimate(flops=2 * slots * rows * kv, bytes_accessed=4 << 20, transcendentals=0),
        compiler_params=pltpu.CompilerParams(vmem_limit_bytes=58 << 20),
        name="rope_and_spread",
    )(select, cosine, sine, rotated)


BLOCK = 1024
PACK = 512


def spread_kernel(select_ref, rows_ref, *rest):
    out_ref, spread = rest[-2:]

    @pl.when(pl.program_id(0) == 0)
    def _():
        spread[...] = one_hot(select_ref[...], spread.shape[1])

    out_ref[...] = jnp.dot(spread[...], rows_ref[...], preferred_element_type=jnp.float32).astype(jnp.bfloat16)


def spread_rows(select, rows, first, width, beside=None):
    slots, count = select.shape[0], rows.shape[0]
    given = [] if beside is None else [beside]
    total = width if beside is None else beside.shape[1]
    return pl.pallas_call(
        spread_kernel,
        grid=(width // PACK,),
        in_specs=[
            pl.BlockSpec((slots, 1), lambda j: (0, 0)),
            pl.BlockSpec((count, PACK), lambda j: (0, first // PACK + j)),
        ]
        + [pl.BlockSpec(memory_space=pl.ANY)] * len(given),
        out_specs=pl.BlockSpec((slots, PACK), lambda j: (0, j)),
        out_shape=jax.ShapeDtypeStruct((slots, total), jnp.bfloat16),
        input_output_aliases={2: 0} if given else {},
        scratch_shapes=[pltpu.VMEM((slots, count), jnp.bfloat16)],
        cost_estimate=pl.CostEstimate(
            flops=2 * slots * count * width, bytes_accessed=2 * (slots + count) * width, transcendentals=0
        ),
        compiler_params=pltpu.CompilerParams(vmem_limit_bytes=58 << 20),
        name="spread_rows",
    )(select, rows, *given)


def lane_sums(values):
    total = values[:, :128]
    for k in range(1, values.shape[1] // 128):
        total = total + values[:, k * 128 : (k + 1) * 128]
    return total


def delta_kernel(core_ref, key_ref, mine_ref, other_ref, gain_ref, out_ref):
    depth = mine_ref.shape[1]
    core = core_ref[0]
    for half, weight_ref in ((core, mine_ref), (1 - core, other_ref)):
        cols = pl.ds(pl.multiple_of(half * depth, depth), depth)
        delta = lax.dot_general(
            key_ref[...], weight_ref[0], (((1,), (1,)), ((), ())), preferred_element_type=jnp.float32
        )
        out_ref[:, cols] = (delta * gain_ref[:, cols]).astype(jnp.bfloat16)


def scaled_delta(core, key_grad, mine, other, gain):
    rows, kv = key_grad.shape
    count, depth = mine.shape[0], mine.shape[1]
    width = gain.shape[1]
    return pl.pallas_call(
        delta_kernel,
        grid_spec=pltpu.PrefetchScalarGridSpec(
            num_scalar_prefetch=1,
            grid=(count,),
            in_specs=[
                pl.BlockSpec((rows, kv), lambda j, core: (0, 0)),
                pl.BlockSpec((1, depth, kv), lambda j, core: (j, 0, 0)),
                pl.BlockSpec((1, depth, kv), lambda j, core: (j, 0, 0)),
                pl.BlockSpec((1, 2 * depth), lambda j, core: (0, j)),
            ],
            out_specs=pl.BlockSpec((rows, 2 * depth), lambda j, core: (0, j)),
        ),
        out_shape=jax.ShapeDtypeStruct((rows, width), jnp.bfloat16),
        cost_estimate=pl.CostEstimate(
            flops=2 * rows * kv * width, bytes_accessed=2 * (rows + kv) * width, transcendentals=0
        ),
        compiler_params=pltpu.CompilerParams(vmem_limit_bytes=58 << 20),
        name="scaled_delta",
    )(core, key_grad, mine, other, gain)


def place_and_sum(gather, arrived_ref, scaled_ref, square_ref, inner_ref):
    values = jnp.dot(gather[...], arrived_ref[...], preferred_element_type=jnp.float32)
    square_ref[...] += lane_sums(values * values)
    inner_ref[...] += lane_sums(scaled_ref[...].astype(jnp.float32) * values)
    return values.astype(jnp.bfloat16)


def first_pass_kernel(select_ref, arrived_ref, scaled_ref, square_in, inner_in, *rest):
    packed_ref, square_ref, inner_ref, gather = rest[-4:]

    @pl.when(pl.program_id(0) == 0)
    def _():
        gather[...] = one_hot(select_ref[...], gather.shape[1])
        square_ref[...] = square_in[...]
        inner_ref[...] = inner_in[...]

    packed_ref[...] = place_and_sum(gather, arrived_ref, scaled_ref, square_ref, inner_ref)


def first_pass(select, arrived, scaled, square, inner, packed, first, part, total):
    rows, slots = select.shape[0], arrived.shape[0]
    base = first // BLOCK
    whole = lambda j: (0, 0)
    column = lambda j: (0, base + j)
    sums = jax.ShapeDtypeStruct((rows, 128), jnp.float32)
    operands = [select, arrived, scaled, square, inner]
    in_specs = [
        pl.BlockSpec((rows, 1), whole),
        pl.BlockSpec((slots, BLOCK), lambda j: (0, j)),
        pl.BlockSpec((rows, BLOCK), column),
        pl.BlockSpec((rows, 128), whole),
        pl.BlockSpec((rows, 128), whole),
    ]
    aliases = {}
    if packed is not None:
        aliases = {len(operands): 0}
        operands.append(packed)
        in_specs.append(pl.BlockSpec(memory_space=pl.ANY))
    return pl.pallas_call(
        first_pass_kernel,
        grid=(part // BLOCK,),
        in_specs=in_specs,
        out_specs=[
            pl.BlockSpec((rows, BLOCK), column),
            pl.BlockSpec((rows, 128), whole),
            pl.BlockSpec((rows, 128), whole),
        ],
        scratch_shapes=[pltpu.VMEM((rows, slots), jnp.bfloat16)],
        out_shape=(jax.ShapeDtypeStruct((rows, total), jnp.bfloat16), sums, sums),
        input_output_aliases=aliases,
        cost_estimate=pl.CostEstimate(
            flops=2 * rows * slots * part, bytes_accessed=(2 * slots + 6 * rows) * part, transcendentals=0
        ),
        compiler_params=pltpu.CompilerParams(vmem_limit_bytes=58 << 20),
        name="first_pass",
    )(*operands)


def last_pass_kernel(
    select_ref, arrived_ref, scaled_ref, packed_ref, square_in, inner_in,
    out_ref, gather, square, inner, inv, coef, kept, kept_scaled, *, early, late, width,
):
    step = pl.program_id(0)

    @pl.when(step == 0)
    def _():
        gather[...] = one_hot(select_ref[...], gather.shape[1])
        square[...] = square_in[...]
        inner[...] = inner_in[...]

    @pl.when(step < late)
    def _():
        kept[step] = place_and_sum(gather, arrived_ref, scaled_ref, square, inner)
        kept_scaled[step] = scaled_ref[...]

    @pl.when(step == late)
    def _():
        inverse = lax.rsqrt(jnp.sum(square[...], axis=1, keepdims=True) * (1.0 / width) + norm_eps)
        inv[...] = inverse
        coef[...] = inverse * inverse * (jnp.sum(inner[...], axis=1, keepdims=True) * (1.0 / width))

    def finish(scaled, values):
        out_ref[...] = (
            inv[...] * (scaled.astype(jnp.float32) - values.astype(jnp.float32) * coef[...])
        ).astype(jnp.bfloat16)

    @pl.when((step >= late) & (step < late + early))
    def _():
        finish(scaled_ref[...], packed_ref[...])

    @pl.when(step >= late + early)
    def _():
        i = step - (late + early)
        finish(kept_scaled[i], kept[i])


def last_pass(select, arrived, scaled, packed, square, inner):
    rows, width = scaled.shape
    slots = arrived.shape[0]
    early, late = packed.shape[1] // BLOCK, arrived.shape[1] // BLOCK
    whole = lambda j: (0, 0)
    return pl.pallas_call(
        functools.partial(last_pass_kernel, early=early, late=late, width=width),
        grid=(2 * late + early,),
        in_specs=[
            pl.BlockSpec((rows, 1), whole),
            pl.BlockSpec((slots, BLOCK), lambda j: (0, jnp.minimum(j, late - 1))),
            pl.BlockSpec(
                (rows, BLOCK), lambda j: (0, jnp.where(j < late, early + j, jnp.minimum(j - late, early - 1)))
            ),
            pl.BlockSpec((rows, BLOCK), lambda j: (0, jnp.clip(j - late, 0, early - 1))),
            pl.BlockSpec((rows, 128), whole),
            pl.BlockSpec((rows, 128), whole),
        ],
        out_specs=pl.BlockSpec((rows, BLOCK), lambda j: (0, jnp.maximum(j - late, 0))),
        scratch_shapes=[
            pltpu.VMEM((rows, slots), jnp.bfloat16),
            pltpu.VMEM((rows, 128), jnp.float32),
            pltpu.VMEM((rows, 128), jnp.float32),
            pltpu.VMEM((rows, 1), jnp.float32),
            pltpu.VMEM((rows, 1), jnp.float32),
            pltpu.VMEM((late, rows, BLOCK), jnp.bfloat16),
            pltpu.VMEM((late, rows, BLOCK), jnp.bfloat16),
        ],
        out_shape=jax.ShapeDtypeStruct((rows, width), jnp.bfloat16),
        cost_estimate=pl.CostEstimate(
            flops=2 * rows * slots * late * BLOCK, bytes_accessed=24 << 20, transcendentals=0
        ),
        compiler_params=pltpu.CompilerParams(vmem_limit_bytes=58 << 20),
        name="last_pass",
    )(select, arrived, scaled, packed, square, inner)


CHUNKS = (3072, 5120)


def body(
    layer_input,
    rotated_grad,
    norm_gain,
    key_weight,
    block_length,
    block_owner,
    block_source_offset,
    block_pack_offset,
    block_position,
):
    tok_rows, width = layer_input.shape
    kv = rotated_grad.shape[1]
    loaders = lax.axis_size("dp")
    columns = lax.axis_size("fsdp")
    dp = lax.axis_index("dp")
    fs = lax.axis_index("fsdp")
    zh, xx, core = dp // 8, (dp // 2) % 4, dp % 2
    yy, zl = fs // 2, fs % 2
    zz = zh * 2 + zl
    capacity = 2 * tok_rows // loaders
    lengths = block_length[0]
    owners = block_owner[0]
    source_offsets = block_source_offset[0]
    pack_offsets = block_pack_offset[0]
    positions = block_position[0]
    shard_ids = jnp.arange(loaders, dtype=jnp.int32)
    slot_ids = jnp.arange(capacity, dtype=jnp.int32)
    row_ids = jnp.arange(tok_rows, dtype=jnp.int32)

    mine = (owners == dp).astype(jnp.int32)
    arrive_start = jnp.sum(mine * pack_offsets, axis=1)
    arrive_length = jnp.sum(mine * lengths, axis=1)
    arrive_position = jnp.sum(mine * positions, axis=1)
    inside = (
        (row_ids[:, None] >= arrive_start[None, :])
        & (row_ids[:, None] < (arrive_start + arrive_length)[None, :])
    ).astype(jnp.int32)
    position = row_ids + jnp.sum(inside * (arrive_position - arrive_start)[None, :], axis=1)
    slot = row_ids + jnp.sum(inside * (shard_ids * capacity - arrive_start)[None, :], axis=1)

    chosen = (pick(owners, dp)[None, :] == shard_ids[:, None]).astype(jnp.int32)
    send_start = jnp.sum(chosen * pick(source_offsets, dp)[None, :], axis=1)
    send_length = jnp.sum(chosen * pick(lengths, dp)[None, :], axis=1)

    def spread(start, length):
        row = jnp.where(slot_ids[None, :] < length[:, None], start[:, None] + slot_ids[None, :], -1)
        return row.reshape(-1)[:, None]

    to_owner = spread(send_start, send_length)
    to_loader = spread(arrive_start, arrive_length)

    def exchange(rows):
        blocks = rows.reshape(loaders, capacity, rows.shape[1])
        return lax.all_to_all(blocks, "dp", split_axis=0, concat_axis=0, tiled=True).reshape(rows.shape)

    depth = key_weight.shape[0] // 2
    half = pick(key_weight.reshape(2, depth, kv), core)
    other_z = swap_zlo(half)

    cosine, sine = rope_tables(position)
    key_grad, message = rope_and_spread(to_loader, cosine, sine, rotated_grad, CHUNKS[0])
    message = spread_rows(to_owner, layer_input, 0, CHUNKS[0], message)
    outgoing = [
        spread_rows(to_owner, layer_input, sum(CHUNKS[:i]), CHUNKS[i]) for i in range(1, len(CHUNKS))
    ]
    message, other_z = lax.optimization_barrier((message, other_z))
    arrived = [exchange(message)]

    pair = jnp.where(zl == 0, jnp.stack([half, other_z]), jnp.stack([other_z, half]))
    mine = jnp.zeros((4, 2, depth, kv), jnp.bfloat16)
    mine = lax.dynamic_update_index_in_dim(mine, pair, yy, 0)
    for n in (1, 3, 2):
        mine = lax.dynamic_update_index_in_dim(mine, along_y(pair, n), (yy - n) % 4, 0)
    mine = mine.reshape(8, depth, kv)
    other = along_core(mine)

    first_in, outgoing[0], later_input, mine, other = lax.optimization_barrier(
        (arrived[0], outgoing[0], layer_input, mine, other)
    )
    arrived[0] = first_in
    for rows_out in outgoing:
        arrived.append(exchange(rows_out))
    key_back = arrived[0][:, CHUNKS[0] :]
    key_loader = lax.dot_general(
        (to_owner == row_ids[None, :]).astype(jnp.bfloat16),
        key_back,
        (((0,), (0,)), ((), ())),
        preferred_element_type=jnp.float32,
    ).astype(jnp.bfloat16)

    gain = norm_gain.astype(jnp.float32)[None, :]
    own = later_input.astype(jnp.float32)
    own_rms = lax.rsqrt(jnp.mean(own * own, axis=-1, keepdims=True) + norm_eps)
    normed = (own * own_rms * gain).astype(jnp.bfloat16)
    scale = 1.0 / math.sqrt(tok_rows * loaders * columns)
    term = (
        lax.dot_general(normed, key_loader, (((0,), (0,)), ((), ())), preferred_element_type=jnp.float32)
        * scale
    ).astype(jnp.bfloat16)
    rows = width // (loaders * columns)
    term = term.reshape(8, 2, 8 * rows, kv)
    got = along_core(pick(term, 1 - core, 1))
    part = (pick(term, core, 1).astype(jnp.float32) + got.astype(jnp.float32)).astype(jnp.bfloat16)

    def reduce(part, axis, me, send):
        total = pick(part, me, axis).astype(jnp.float32)
        for n in (1, 3, 2):
            total = total + send(pick(part, (me + n) % 4, axis), n).astype(jnp.float32)
        return total

    part = reduce(part.reshape(8, 4, 2 * rows, kv), 1, yy, along_y).astype(jnp.bfloat16)
    core_id = jnp.reshape(core, (1,)).astype(jnp.int32)
    select = slot[:, None]
    square = jnp.zeros((tok_rows, 128), jnp.float32)
    inner = jnp.zeros((tok_rows, 128), jnp.float32)
    scaled = scaled_delta(core_id, key_grad, mine, other, gain)
    packed, first = None, 0
    for rows_in, size in zip(arrived[:-1], CHUNKS[:-1]):
        packed, square, inner = first_pass(
            select, rows_in, scaled, square, inner, packed, first, size, sum(CHUNKS[:-1])
        )
        first += size
    part, square, inner = lax.optimization_barrier((part, square, inner))
    part = part.reshape(2, 4, 2, rows, kv).transpose(0, 2, 1, 3, 4).reshape(4, 4, rows, kv)
    part = reduce(part, 0, zz, along_z).astype(jnp.bfloat16)
    kept = pick(part, xx)
    pieces = [along_x(pick(part, (xx + n) % 4), n) for n in (1, 3, 2)]

    input_grad = last_pass(select, arrived[-1], scaled, packed, square, inner)
    input_grad, kept, pieces = lax.optimization_barrier((input_grad, kept, pieces))
    weight_grad = kept.astype(jnp.float32)
    for piece in pieces:
        weight_grad = weight_grad + piece.astype(jnp.float32)
    return (input_grad, weight_grad)


def solution(mesh):
    return jax.shard_map(
        body,
        mesh=mesh,
        in_specs=(
            P(("dp", "fsdp"), None),
            P(("dp", "fsdp"), None),
            P(),
            P("fsdp", None),
            P("fsdp", None, None),
            P("fsdp", None, None),
            P("fsdp", None, None),
            P("fsdp", None, None),
            P("fsdp", None, None),
        ),
        out_specs=(P(("dp", "fsdp"), None), P(("dp", "fsdp"), None)),
        check_vma=False,
    )
```
